256 devices in a mesh: nodes: 256 (over x, y, z, core).
Axes of the slice: x: 4, y: 4, z: 8, core: 2. Of those that a mesh axis runs over, the one named last changes fastest.
Arguments:
- node_q: bfloat16 [131072, 512], P('nodes'), may hold values from -6 to 6
- node_k: bfloat16 [131072, 512], P('nodes'), may hold values from -6 to 6
- node_v: bfloat16 [131072, 512], P('nodes'), may hold values from -5 to 5
- node_grad: bfloat16 [131072, 512], P('nodes'), may hold values from -5 to 5
- local_cols: int32 [1024, 4], P('nodes'), may hold values from 0 to 1023, as said below
- expander_cols: int32 [1024, 2], P('nodes'), may hold values from 0 to 1023, as said below
- edge_bits: int32 [1024, 6, 8], P('nodes'), may hold values from -2147483648 to 2147483646
- virt_q: bfloat16 [64, 512], replicated, may hold values from -6 to 6
- virt_k: bfloat16 [64, 512], replicated, may hold values from -6 to 6
- virt_v: bfloat16 [64, 512], replicated, may hold values from -5 to 5
- virt_grad: bfloat16 [64, 512], replicated, may hold values from -5 to 5
Outputs:
- node_output: bfloat16 [131072, 512], P('nodes')
- virtual_output: bfloat16 [64, 512], replicated
- grad_q: bfloat16 [131072, 512], P('nodes')
- grad_k: bfloat16 [131072, 512], P('nodes')
- grad_v: bfloat16 [131072, 512], P('nodes')
- grad_vq: bfloat16 [64, 512], replicated
- grad_vk: bfloat16 [64, 512], replicated
- grad_vv: bfloat16 [64, 512], replicated
The draws below stay inside these ranges and needn't reach their ends.
Inputs may be any that keep to these rules, and one draw needn't show every extreme that they name: local_cols[b, 0] = b, and every local entry lies within 2 blocks of b. `expander_cols`: let block b be the r-th of the 4 blocks of device p = b // 4, and j = r * 2 + e. Expander entry e of block b is a block of device (p + n / 2 ** (j mod 5 + 1)) mod n, n the number of devices.
All inputs are finite; a program needn't handle non-finite values.
Results may differ from the reference program's by a relative error of at most 0.034.
Values may be sent and summed in bfloat16 or wider, within the bound.
No kernel may reach another device: no remote copies, remote signals or barrier semaphores. Data moves between devices by JAX's collectives and lax.ppermute only.
A program may use at most 256 MiB of HBM per device.

```python
import math
import jax
import jax.numpy as jnp
from jax import lax

D = 512
HEADS = 8
BLK = 128
NB = 4
LOC = 4
EXP = 2
OFFS = 5
VIRTUAL_COUNT = 64
REACH = 2
NBLK = 1024
NODES = 131072


def drawn_normal(key, shape):
    return jnp.clip(jax.random.normal(key, shape, jnp.float32), -5.0, 5.0)


def draw_node_q(key, part):
    key = jax.random.fold_in(key, 11)
    values = drawn_normal(key, (NODES, D))
    return values.astype(jnp.bfloat16)


def draw_node_k(key, part):
    key = jax.random.fold_in(key, 12)
    values = drawn_normal(key, (NODES, D))
    return values.astype(jnp.bfloat16)


def draw_virt_q(key, part):
    key = jax.random.fold_in(key, 13)
    values = drawn_normal(key, (VIRTUAL_COUNT, D))
    return values.astype(jnp.bfloat16)


def draw_virt_k(key, part):
    key = jax.random.fold_in(key, 14)
    values = drawn_normal(key, (VIRTUAL_COUNT, D))
    return values.astype(jnp.bfloat16)


def draw_local_cols(key, part):
    key = jax.random.fold_in(key, 15)
    offsets = jax.random.randint(key, (NBLK, LOC), -REACH, REACH + 1, dtype=jnp.int32)
    offsets = offsets.at[:, 0].set(0)
    base_rows = jnp.arange(NBLK, dtype=jnp.int32)[:, None]
    return jnp.clip(base_rows + offsets, 0, NBLK - 1).astype(jnp.int32)


def draw_expander_cols(key, part):
    key = jax.random.fold_in(key, 16)
    devices = NBLK // NB
    all_blocks = jnp.arange(NBLK, dtype=jnp.int32)
    owner = all_blocks // NB
    local_row = all_blocks % NB
    entry = jnp.arange(EXP, dtype=jnp.int32)
    order = local_row[:, None] * EXP + entry[None, :]
    turn = order % OFFS
    distance = jnp.right_shift(jnp.int32(devices), turn + 1)
    target = (owner[:, None] + distance) % devices
    within = jax.random.randint(key, (NBLK, EXP), 0, NB, dtype=jnp.int32)
    return (target * NB + within).astype(jnp.int32)


def with_ends(drawn, rng, smallest, top_value):
    place = [jax.random.randint(jax.random.fold_in(rng, axis), (), 0, length) for axis, length in enumerate(drawn.shape)]
    main_axis = drawn.shape.index(max(drawn.shape))
    beside = place[:main_axis] + [(place[main_axis] + 1) % drawn.shape[main_axis]] + place[main_axis + 1:]
    return drawn.at[tuple(place)].set(smallest).at[tuple(beside)].set(top_value)


def steps_of(rng, shape, shards, smallest, largest):
    level, own = 1.0, jax.random.fold_in(rng, 6)
    for axis_at, parts in shards:
        steps = jnp.exp(jax.random.uniform(jax.random.fold_in(own, axis_at), (parts,), jnp.float32, smallest / len(shards), largest / len(shards)))
        level = level * jnp.repeat(steps, shape[axis_at] // parts).reshape([-1 if axis == axis_at else 1 for axis in range(len(shape))])
    return level


def bell_draw(rng, shape, scale, limit, cuts=(), kind=jnp.bfloat16):
    result = scale * jax.random.normal(rng, shape, jnp.float32)
    if cuts:
        result = result * steps_of(rng, shape, cuts, -0.22, 0.18)
    return jnp.clip(result, -limit, limit).astype(kind)


def setup_inputs(seed: int = 0) -> dict:
    key_list = jax.random.split(jax.random.key(seed), 12)
    node_q = draw_node_q(jax.random.fold_in(key_list[11], 71), 0)
    node_k = draw_node_k(jax.random.fold_in(key_list[11], 71), 0)
    node_v = bell_draw(key_list[2], (NODES, D), 1.0, 5.0, ((0, 256),))
    node_grad = bell_draw(key_list[3], (NODES, D), 1.0, 5.0, ((0, 256),))
    local_cols = draw_local_cols(jax.random.fold_in(key_list[11], 71), 0)
    expander_cols = draw_expander_cols(jax.random.fold_in(key_list[11], 71), 0)
    edge_bits = with_ends(jax.random.randint(key_list[6], (NBLK, LOC + EXP, 2 * BLK // 32), -2147483648, 2147483647), jax.random.fold_in(key_list[6], 1), -2147483648, 2147483646).astype(jnp.int32)
    virt_q = draw_virt_q(jax.random.fold_in(key_list[11], 71), 0)
    virt_k = draw_virt_k(jax.random.fold_in(key_list[11], 71), 0)
    virt_v = bell_draw(key_list[9], (VIRTUAL_COUNT, D), 1.0, 5.0)
    virt_grad = bell_draw(key_list[10], (VIRTUAL_COUNT, D), 1.0, 5.0)
    return dict(node_q=node_q, node_k=node_k, node_v=node_v, node_grad=node_grad, local_cols=local_cols, expander_cols=expander_cols, edge_bits=edge_bits, virt_q=virt_q, virt_k=virt_k, virt_v=virt_v, virt_grad=virt_grad)


highest = lax.Precision.HIGHEST

def unpack_bits(words):
    shifts = jnp.arange(32, dtype=jnp.int32)
    bits = jnp.right_shift(words[..., None], shifts) & 1
    return bits.reshape(words.shape[:-1] + (words.shape[-1] * 32,))

def matrix_product(form, left, right):
    return jnp.einsum(form, left.astype(jnp.float32), right.astype(jnp.float32), precision=highest)

def block_pass(query_rows, grad_out, keys, values, words, virt_keys, virt_values, score_scale):
    width_rows = query_rows.shape[0]
    slots = words.shape[0]
    unpacked = unpack_bits(words)
    mask = unpacked[:, :width_rows, None] * unpacked[:, None, width_rows:] > 0
    mask = jnp.transpose(mask, (1, 0, 2)).reshape(width_rows, slots * width_rows)[None]
    scores = matrix_product('qhd,khd->hqk', query_rows, keys) * score_scale
    virt_scores = matrix_product('qhd,vhd->hqv', query_rows, virt_keys) * score_scale
    row_max = jnp.maximum(lax.optimization_barrier(jnp.max(jnp.where(mask, scores, -1e+30), axis=-1)), lax.optimization_barrier(jnp.max(virt_scores, axis=-1)))
    edge_w = jnp.where(mask, jnp.exp(scores - row_max[..., None]), 0.0)
    virt_w = jnp.exp(virt_scores - row_max[..., None])
    total = lax.optimization_barrier(jnp.sum(edge_w, axis=-1)) + lax.optimization_barrier(jnp.sum(virt_w, axis=-1))
    summed = matrix_product('hqk,khd->qhd', edge_w.astype(jnp.bfloat16), values)
    summed = summed + matrix_product('hqv,vhd->qhd', virt_w.astype(jnp.bfloat16), virt_values)
    node_output = (summed / total.T[:, :, None]).astype(jnp.bfloat16)
    delta = lax.optimization_barrier(jnp.sum(grad_out.astype(jnp.float32) * node_output.astype(jnp.float32), axis=-1)).T
    edge_p = edge_w / total[..., None]
    virt_p = virt_w / total[..., None]
    value_gradient_rows = matrix_product('hqk,qhd->khd', edge_p.astype(jnp.bfloat16), grad_out)
    edge_ds = (edge_p * (matrix_product('qhd,khd->hqk', grad_out, values) - delta[..., None])).astype(jnp.bfloat16)
    virtual_score_gradient = virt_p * (matrix_product('qhd,vhd->hqv', grad_out, virt_values) - delta[..., None])
    query_gradient = (matrix_product('hqk,khd->qhd', edge_ds, keys) + matrix_product('hqv,vhd->qhd', virtual_score_gradient, virt_keys)) * score_scale
    key_gradient_rows = matrix_product('hqk,qhd->khd', edge_ds, query_rows) * score_scale
    virtual_key_gradient_rows = matrix_product('bmp,mbl->pbl', virtual_score_gradient, query_rows) * score_scale
    virtual_value_gradient_rows = matrix_product('bmp,mbl->pbl', virt_p, grad_out)
    return (node_output, query_gradient, key_gradient_rows, value_gradient_rows, virtual_key_gradient_rows, virtual_value_gradient_rows)

def reference(node_q, node_k, node_v, node_grad, local_cols, expander_cols, edge_bits, virt_q, virt_k, virt_v, virt_grad):
    node_indices, block_width = node_q.shape
    head_dim = block_width // HEADS
    blocks = node_indices // BLK
    score_scale = 1.0 / math.sqrt(head_dim)
    block_shape = (blocks, BLK, HEADS, head_dim)
    query_blocks = node_q.reshape(block_shape)
    key_blocks = node_k.reshape(block_shape)
    value_blocks = node_v.reshape(block_shape)
    grad_blocks = node_grad.reshape(block_shape)
    columns = jnp.concatenate([local_cols, expander_cols], axis=1).astype(jnp.int32)
    slots = columns.shape[1]
    virt_queries = virt_q.reshape(VIRTUAL_COUNT, HEADS, head_dim)
    virt_keys = virt_k.reshape(VIRTUAL_COUNT, HEADS, head_dim)
    virt_values = virt_v.reshape(VIRTUAL_COUNT, HEADS, head_dim)
    virt_grads = virt_grad.reshape(VIRTUAL_COUNT, HEADS, head_dim)

    def step(loop_state, index):
        key_gradients, value_gradients, virtual_key_sum, virtual_value_sum = loop_state
        chosen = columns[index]
        keys = jnp.take(key_blocks, chosen, axis=0).reshape(slots * BLK, HEADS, head_dim)
        values = jnp.take(value_blocks, chosen, axis=0).reshape(slots * BLK, HEADS, head_dim)
        result_list = block_pass(query_blocks[index], grad_blocks[index], keys, values, edge_bits[index], virt_keys, virt_values, score_scale)
        node_output, query_gradient, key_gradient_rows, value_gradient_rows, virtual_key_gradient_rows, virtual_value_gradient_rows = result_list
        key_gradients = key_gradients.at[chosen].add(key_gradient_rows.reshape(slots, BLK, HEADS, head_dim))
        value_gradients = value_gradients.at[chosen].add(value_gradient_rows.reshape(slots, BLK, HEADS, head_dim))
        return ((key_gradients, value_gradients, virtual_key_sum + virtual_key_gradient_rows, virtual_value_sum + virtual_value_gradient_rows), (node_output, query_gradient))
    start = (jnp.zeros(block_shape, jnp.float32), jnp.zeros(block_shape, jnp.float32), jnp.zeros((VIRTUAL_COUNT, HEADS, head_dim), jnp.float32), jnp.zeros((VIRTUAL_COUNT, HEADS, head_dim), jnp.float32))
    carried_state, stacked = lax.scan(step, start, jnp.arange(blocks, dtype=jnp.int32))
    key_gradients, value_gradients, virtual_key_sum, virtual_value_sum = carried_state
    node_output_rows, query_gradients = stacked
    flat_keys = node_k.reshape(node_indices, HEADS, head_dim)
    flat_values = node_v.reshape(node_indices, HEADS, head_dim)
    virt_scores = matrix_product('uhd,nhd->hun', virt_queries, flat_keys) * score_scale
    virt_top = lax.optimization_barrier(jnp.max(virt_scores, axis=-1))
    weights = jnp.exp(virt_scores - virt_top[..., None])
    virt_total = lax.optimization_barrier(jnp.sum(weights, axis=-1))
    virtual_output = (matrix_product('hun,nhd->uhd', weights, flat_values) / virt_total.T[:, :, None]).astype(jnp.bfloat16)
    virt_delta = lax.optimization_barrier(jnp.sum(virt_grads.astype(jnp.float32) * virtual_output.astype(jnp.float32), axis=-1)).T
    virt_prob = weights / virt_total[..., None]
    node_dv = matrix_product('hun,uhd->nhd', virt_prob, virt_grads)
    virt_dscore = virt_prob * (matrix_product('uhd,nhd->hun', virt_grads, flat_values) - virt_delta[..., None])
    virtual_query_gradient = matrix_product('hun,nhd->uhd', virt_dscore, flat_keys) * score_scale
    node_dk = matrix_product('hun,uhd->nhd', virt_dscore, virt_queries) * score_scale
    key_gradient_total = (key_gradients.reshape(node_indices, block_width) + node_dk.reshape(node_indices, block_width)).astype(jnp.bfloat16)
    value_gradient_total = (value_gradients.reshape(node_indices, block_width) + node_dv.reshape(node_indices, block_width)).astype(jnp.bfloat16)
    return (node_output_rows.reshape(node_indices, block_width), virtual_output.reshape(VIRTUAL_COUNT, block_width), query_gradients.reshape(node_indices, block_width).astype(jnp.bfloat16), key_gradient_total, value_gradient_total, virtual_query_gradient.reshape(VIRTUAL_COUNT, block_width).astype(jnp.bfloat16), virtual_key_sum.reshape(VIRTUAL_COUNT, block_width).astype(jnp.bfloat16), virtual_value_sum.reshape(VIRTUAL_COUNT, block_width).astype(jnp.bfloat16))
```

```python
import functools
import math

import jax
import jax.numpy as jnp
from jax import lax
from jax.experimental import pallas as pl
from jax.experimental.pallas import tpu as pltpu
from jax.sharding import PartitionSpec as P

HEADS = 8
HD = 64
BLK = 128
NB = 4
LOC = 4
EXP = 2
OFFS = 5
VC = 64
REACH = 2
D = HEADS * HD
ROWS = NB * BLK
PAIRS = HEADS // 2
FAR = NB * EXP
COLS = (LOC + EXP) * BLK
ALL = COLS + VC
BAND = NB + 2 * REACH
SCALE = 1.0 / math.sqrt(HD)
MASKED = -1e30
F32 = jnp.float32
BF16 = jnp.bfloat16
COUNTS = [len(range(turn, FAR, OFFS)) for turn in range(OFFS)]


def dot(left, right, contract):
    return lax.dot_general(
        left, right, ((contract[:1], contract[1:]), ((), ())), preferred_element_type=F32
    )


def nn(left, right):
    return dot(left, right, (1, 0))


def nt(left, right):
    return dot(left, right, (1, 1))


def tn(left, right):
    return dot(left, right, (0, 0))


def split_pair(cells):
    low = lax.broadcasted_iota(jnp.int32, cells.shape, 1) < HD
    zero = jnp.zeros_like(cells)
    return jnp.concatenate([jnp.where(low, cells, zero), jnp.where(low, zero, cells)], axis=0)


def lanes(pair):
    return slice(pair * 2 * HD, (pair + 1) * 2 * HD)


def virtual_sums_kernel(k_ref, v_ref, vq_ref, vg_ref, out_ref):
    for pair in range(PAIRS):
        sl = lanes(pair)
        keys, values = k_ref[:, sl], v_ref[:, sl]
        wq = split_pair(vq_ref[:, sl] * SCALE).astype(BF16)
        wg = split_pair(vg_ref[:, sl])
        scores = nt(keys, wq)
        top = jnp.max(scores, axis=0, keepdims=True)
        p = jnp.exp(scores - top)
        total = jnp.sum(p, axis=0, keepdims=True)
        gv = nt(values, wg)
        centre = jnp.sum(p * gv, axis=0, keepdims=True) / total
        rounded = p.astype(BF16)
        weighted = tn(rounded, values)
        first = tn((p * (gv - centre)).astype(BF16), keys)
        second = tn(rounded, keys)
        stats = jnp.concatenate(
            [top, total, centre, jnp.zeros((2 * VC - 3, 2 * VC), F32)], axis=0
        ).T
        for half in range(2):
            rows = slice(half * VC, (half + 1) * VC)
            part = slice(half * HD, (half + 1) * HD)
            at = pair * 2 * VC + half * VC
            base = (at // 256) * 256
            dst = slice(at % 256, at % 256 + VC)
            out_ref[dst, base : base + 128] = jnp.concatenate(
                [weighted[rows, part], stats[rows, :HD]], axis=1
            )
            out_ref[dst, base + 128 : base + 256] = jnp.concatenate(
                [first[rows, part], second[rows, part]], axis=1
            )


def virtual_merge_kernel(parts_ref, grad_ref, out_ref):
    for c in range(2):
        base = c * 256
        one = parts_ref[:, base : base + 128]
        two = parts_ref[:, base + 128 : base + 256]
        top, total, centre = (one[:, HD + n : HD + n + 1] for n in range(3))
        highest = jnp.max(top, axis=0, keepdims=True)
        scale = jnp.exp(top - highest)
        all_total = jnp.sum(scale * total, axis=0, keepdims=True)
        output = jnp.sum(scale * one[:, :HD], axis=0, keepdims=True) / all_total
        output = output.astype(BF16).astype(F32)
        vdelta = jnp.sum(grad_ref[c : c + 1, :] * output, axis=1, keepdims=True)
        grad = jnp.sum(
            scale * (two[:, :HD] + (centre - vdelta) * two[:, HD:]), axis=0, keepdims=True
        )
        grad = grad * (SCALE / all_total)
        lane = lax.broadcasted_iota(jnp.int32, (1, 128), 1)
        stats = jnp.where(lane == 0, highest, jnp.where(lane == 1, all_total, vdelta))
        result = jnp.concatenate([output, grad, stats], axis=1)
        out_ref[:, base : base + 256] = jnp.broadcast_to(result, (out_ref.shape[0], 256))


def pack_kernel(wanted_ref, k_ref, v_ref, *rest):
    outs, sem = rest[:OFFS], rest[OFFS]
    copies = []
    for member in range(FAR):
        turn, slot = member % OFFS, member // OFFS
        start = pl.multiple_of(wanted_ref[member] * BLK, BLK)
        for which, ref in enumerate((k_ref, v_ref)):
            copies.append(
                pltpu.make_async_copy(
                    ref.at[pl.ds(start, BLK)], outs[turn].at[slot, which], sem.at[len(copies)]
                )
            )
    for copy in copies:
        copy.start()
    for copy in copies:
        copy.wait()


def edges_kernel(
    place_ref,
    bits_ref,
    q_ref,
    g_ref,
    k_ref,
    v_ref,
    left_ref,
    right_ref,
    vq_ref,
    vk_ref,
    vv_ref,
    vg_ref,
    all_ref,
    far0,
    far1,
    far2,
    far3,
    far4,
    out_ref,
    gq_ref,
    own_ref,
    to_left_ref,
    to_right_ref,
    sums_ref,
    vout_ref,
    gvq_ref,
    fg0,
    fg1,
    fg2,
    fg3,
    fg4,
    band,
    far,
    far_grads,
    cat,
    bias,
    acc,
    virt_acc,
    sem,
):
    fars = (far0, far1, far2, far3, far4)
    far_outs = (fg0, fg1, fg2, fg3, fg4)
    arrivals = [
        pltpu.make_async_copy(fars[m % OFFS].at[m // OFFS], far.at[m], sem.at[m])
        for m in range(FAR)
    ]
    for copy in arrivals:
        copy.start()
    edge = REACH * BLK
    for which, own in enumerate((k_ref, v_ref)):
        band[which, 0:edge] = left_ref[which]
        band[which, edge : edge + ROWS] = own[...]
        band[which, edge + ROWS : 2 * edge + ROWS] = right_ref[which]
        acc[which, 0:edge] = jnp.zeros((edge, D), F32)
        acc[which, edge + ROWS : 2 * edge + ROWS] = jnp.zeros((edge, D), F32)
    cat[0, COLS:ALL] = vk_ref[...]
    cat[1, COLS:ALL] = vv_ref[...]
    bias[COLS:ALL] = jnp.zeros((VC, 2 * BLK), F32)
    virt_acc[...] = jnp.zeros(virt_acc.shape, F32)

    for head in range(HEADS):
        at = slice((head % 4) * VC, (head % 4 + 1) * VC)
        base = (head // 4) * 256
        cells = all_ref[at, base : base + 128]
        vout_ref[:, head * HD : (head + 1) * HD] = cells[:, :HD].astype(BF16)
        gvq_ref[:, head * HD : (head + 1) * HD] = cells[:, HD:].astype(BF16)
    for pair in range(PAIRS):
        sl = lanes(pair)
        at = pair * 2 * VC
        base = (at // 256) * 256
        stats = all_ref[at % 256 : at % 256 + 2 * VC, base + 128 : base + 256].T
        top, total, vdelta = stats[0:1], stats[1:2], stats[2:3]
        wq = split_pair(vq_ref[:, sl] * SCALE).astype(BF16)
        wg = split_pair(vg_ref[:, sl])
        p = jnp.exp(nt(k_ref[:, sl], wq) - top) * (1.0 / total)
        da = p * (nt(v_ref[:, sl], wg) - vdelta)
        acc[0, edge : edge + ROWS, sl] = nn(da.astype(BF16), wq)
        acc[1, edge : edge + ROWS, sl] = nn(p.astype(BF16), wg)

    for copy in arrivals:
        copy.wait()

    row_lane = lax.broadcasted_iota(jnp.int32, (1, 2 * BLK), 1) % BLK
    col_row = lax.broadcasted_iota(jnp.int32, (BLK, 2 * BLK), 0)

    def pick(words, index):
        word = index // 32
        chosen = jnp.where(
            word == 0, words[0], jnp.where(word == 1, words[1], jnp.where(word == 2, words[2], words[3]))
        )
        return (jnp.right_shift(chosen, index % 32) & 1) > 0

    def row_block(b, carry):
        rows = pl.ds(pl.multiple_of(b * BLK, BLK), BLK)
        places = [pl.multiple_of(place_ref[b, e] * BLK, BLK) for e in range(LOC)]
        for e in range(LOC + EXP):
            at = slice(e * BLK, (e + 1) * BLK)
            for which in range(2):
                if e < LOC:
                    cat[which, at] = band[which, pl.ds(places[e], BLK)]
                else:
                    cat[which, at] = far[b * EXP + (e - LOC), which]
            words = [bits_ref[b, e * 8 + w] for w in range(8)]
            linked = pick(words[:4], row_lane) & pick(words[4:], col_row)
            bias[at] = jnp.where(linked, 0.0, MASKED)
        for pair in range(PAIRS):
            sl = lanes(pair)
            grad = g_ref[rows, sl]
            wq = split_pair(q_ref[rows, sl] * SCALE).astype(BF16)
            wg = split_pair(grad)
            keys, values = cat[0, :, sl], cat[1, :, sl]
            scores = nt(keys, wq) + bias[...]
            top = jnp.max(scores, axis=0, keepdims=True)
            w = jnp.exp(scores - top)
            total = jnp.sum(w, axis=0, keepdims=True)
            p = w * (1.0 / total)
            rounded = p.astype(BF16)
            mixed = tn(values, rounded)
            output = jnp.concatenate([mixed[:HD, :BLK], mixed[HD:, BLK:]], axis=0)
            output = output.astype(BF16).astype(F32)
            out_ref[rows, sl] = output.T.astype(BF16)
            product = output * grad.astype(F32).T
            delta = jnp.concatenate(
                [
                    jnp.sum(product[:HD], axis=0, keepdims=True),
                    jnp.sum(product[HD:], axis=0, keepdims=True),
                ],
                axis=1,
            )
            ds = (p * (nt(values, wg) - delta)).astype(BF16)
            mixed = tn(keys, ds)
            grad_q = jnp.concatenate([mixed[:HD, :BLK], mixed[HD:, BLK:]], axis=0)
            gq_ref[rows, sl] = (grad_q * SCALE).T.astype(BF16)
            for which, grads in enumerate((nn(ds, wq), nn(rounded, wg))):
                for e in range(LOC):
                    acc[which, pl.ds(places[e], BLK), sl] += grads[e * BLK : (e + 1) * BLK]
                for e in range(EXP):
                    at = slice((LOC + e) * BLK, (LOC + e + 1) * BLK)
                    far_grads[b * EXP + e, which, :, sl] = grads[at].astype(BF16)
                virt_acc[which, :, sl] += grads[COLS:]
        return carry

    lax.fori_loop(0, NB, row_block, 0)

    leaving = [
        pltpu.make_async_copy(far_grads.at[m], far_outs[m % OFFS].at[m // OFFS], sem.at[m])
        for m in range(FAR)
    ]
    for copy in leaving:
        copy.start()
    for which in range(2):
        to_left_ref[which] = acc[which, 0:edge].astype(BF16)
        own_ref[which] = acc[which, edge : edge + ROWS]
        to_right_ref[which] = acc[which, edge + ROWS : 2 * edge + ROWS].astype(BF16)
        for half in range(2):
            at = half * 2 * VC + which * VC
            sums_ref[at : at + VC, :] = virt_acc[which, :, half * 256 : (half + 1) * 256]
    for copy in leaving:
        copy.wait()


def collect_kernel(
    wanted_ref, own_ref, from_left_ref, from_right_ref, far0, far1, far2, far3, far4, gk_ref, gv_ref, acc
):
    fars = (far0, far1, far2, far3, far4)
    edge = REACH * BLK
    for which in range(2):
        acc[which, 0:edge] = own_ref[which, 0:edge] + from_left_ref[which].astype(F32)
        acc[which, edge:ROWS] = own_ref[which, edge:ROWS] + from_right_ref[which].astype(F32)
    for member in range(FAR):
        start = pl.multiple_of(wanted_ref[member] * BLK, BLK)
        for which in range(2):
            acc[which, pl.ds(start, BLK)] += fars[member % OFFS][member // OFFS, which].astype(F32)
    gk_ref[...] = acc[0].astype(BF16)
    gv_ref[...] = acc[1].astype(BF16)


def vmem(count):
    return [pl.BlockSpec(memory_space=pltpu.VMEM)] * count


def smem(count):
    return [pl.BlockSpec(memory_space=pltpu.SMEM)] * count


def anywhere(count):
    return [pl.BlockSpec(memory_space=pl.ANY)] * count


def shape(dims, dtype):
    return jax.ShapeDtypeStruct(dims, dtype)


def call(kernel, name, ins, outs, out_specs, scratch=(), flops=0, moved=0, limit=48):
    return pl.pallas_call(
        kernel,
        out_shape=outs,
        in_specs=ins,
        out_specs=out_specs,
        scratch_shapes=list(scratch),
        name=name,
        cost_estimate=pl.CostEstimate(flops=flops, bytes_accessed=moved, transcendentals=0),
        compiler_params=pltpu.CompilerParams(vmem_limit_bytes=limit * 2**20),
    )


def shift(cells, distance):
    count = lax.axis_size("nodes")
    return lax.ppermute(cells, "nodes", [(i, (i + distance) % count) for i in range(count)])


def exchange(cells):
    return lax.all_to_all(cells, "nodes", 0, 0, tiled=True)


def on_device(
    node_q,
    node_k,
    node_v,
    node_grad,
    local_cols,
    expander_cols,
    edge_bits,
    virt_q,
    virt_k,
    virt_v,
    virt_grad,
):
    devices = lax.axis_size("nodes")
    me = lax.axis_index("nodes")
    edge = REACH * BLK
    distances = [devices >> (turn + 1) for turn in range(OFFS)]

    requests = [shift(expander_cols, distance) for distance in distances]
    wanted = jnp.stack(
        [requests[m % OFFS].reshape(FAR)[m] % NB for m in range(FAR)]
    )
    from_left = shift(jnp.stack([node_k[ROWS - edge :], node_v[ROWS - edge :]]), 1)
    from_right = shift(jnp.stack([node_k[:edge], node_v[:edge]]), -1)

    packed_shapes = [shape((count, 2, BLK, D), BF16) for count in COUNTS]
    packed = call(
        pack_kernel,
        "pack_wanted",
        smem(1) + anywhere(2),
        packed_shapes,
        anywhere(OFFS),
        [pltpu.SemaphoreType.DMA((2 * FAR,))],
        moved=4 * 2**20,
        limit=16,
    )(wanted, node_k, node_v)
    far = [shift(cells, -distance) for cells, distance in zip(packed, distances)]

    parts = call(
        virtual_sums_kernel,
        "virtual_sums",
        vmem(4),
        shape((devices, 512), F32),
        pl.BlockSpec(memory_space=pltpu.VMEM),
        flops=2 * ROWS * VC * D * 5,
        moved=2 * 2**20,
    )(node_k, node_v, virt_q, virt_grad)
    parts = exchange(parts)
    first = lax.dynamic_slice(virt_grad, (me % VC, (me // VC) * HD), (1, HD))
    second = lax.dynamic_slice(virt_grad, (me % VC, (me // VC + HEADS // 2) * HD), (1, HD))
    columns = jnp.concatenate([first, second], axis=0).astype(F32)
    merged = call(
        virtual_merge_kernel,
        "virtual_merge",
        vmem(2),
        shape((devices, 512), F32),
        pl.BlockSpec(memory_space=pltpu.VMEM),
        flops=2**20,
        moved=2**20,
    )(parts, columns)
    merged = exchange(merged)

    places = local_cols - me * NB + REACH
    outs = call(
        edges_kernel,
        "edges",
        smem(2) + vmem(11) + anywhere(OFFS),
        [
            shape((ROWS, D), BF16),
            shape((ROWS, D), BF16),
            shape((2, ROWS, D), F32),
            shape((2, edge, D), BF16),
            shape((2, edge, D), BF16),
            shape((devices, 256), F32),
            shape((VC, D), BF16),
            shape((VC, D), BF16),
        ]
        + packed_shapes,
        vmem(8) + anywhere(OFFS),
        [
            pltpu.VMEM((2, BAND * BLK, D), BF16),
            pltpu.VMEM((FAR, 2, BLK, D), BF16),
            pltpu.VMEM((FAR, 2, BLK, D), BF16),
            pltpu.VMEM((2, ALL, D), BF16),
            pltpu.VMEM((ALL, 2 * BLK), F32),
            pltpu.VMEM((2, BAND * BLK, D), F32),
            pltpu.VMEM((2, VC, D), F32),
            pltpu.SemaphoreType.DMA((FAR,)),
        ],
        flops=2 * ROWS * ALL * D * 6,
        moved=12 * 2**20,
        limit=56,
    )(
        places,
        edge_bits.reshape(NB, (LOC + EXP) * 8),
        node_q,
        node_grad,
        node_k,
        node_v,
        from_left,
        from_right,
        virt_q,
        virt_k,
        virt_v,
        virt_grad,
        merged,
        *far,
    )
    node_output, grad_q, own, to_left, to_right, sums, virtual_output, grad_vq = outs[:8]
    returned = [shift(cells, distance) for cells, distance in zip(outs[8:], distances)]
    from_right_grads = shift(to_left, -1)
    from_left_grads = shift(to_right, 1)

    sums = exchange(sums)
    sums = jnp.sum(sums, axis=0, keepdims=True)
    sums = exchange(jnp.broadcast_to(sums, (devices, 256)))
    sums = sums.reshape(2, 2, VC, 256)
    grad_vk = jnp.concatenate([sums[0, 0], sums[1, 0]], axis=1).astype(BF16)
    grad_vv = jnp.concatenate([sums[0, 1], sums[1, 1]], axis=1).astype(BF16)

    grad_k, grad_v = call(
        collect_kernel,
        "collect",
        smem(1) + vmem(3 + OFFS),
        [shape((ROWS, D), BF16)] * 2,
        vmem(2),
        [pltpu.VMEM((2, ROWS, D), F32)],
        flops=2**20,
        moved=6 * 2**20,
    )(wanted, own, from_left_grads, from_right_grads, *returned)
    return node_output, virtual_output, grad_q, grad_k, grad_v, grad_vq, grad_vk, grad_vv


def solution(mesh):
    rows = P("nodes", None)
    return jax.shard_map(
        on_device,
        mesh=mesh,
        in_specs=(rows,) * 6 + (P("nodes", None, None),) + (P(),) * 4,
        out_specs=(rows, P(), rows, rows, rows, P(), P(), P()),
        check_vma=False,
    )
```

```python
import functools
import math

import jax
import jax.numpy as jnp
from jax import lax
from jax.experimental import pallas as pl
from jax.experimental.pallas import tpu as pltpu
from jax.sharding import PartitionSpec as P

HEADS = 8
HD = 64
BLK = 128
NB = 4
LOC = 4
EXP = 2
OFFS = 5
VC = 64
REACH = 2
D = HEADS * HD
ROWS = NB * BLK
PAIRS = HEADS // 2
FAR = NB * EXP
COLS = (LOC + EXP) * BLK
ALL = COLS + VC
BAND = NB + 2 * REACH
SCALE = 1.0 / math.sqrt(HD)
MASKED = -1e30
F32 = jnp.float32
BF16 = jnp.bfloat16
COUNTS = [len(range(turn, FAR, OFFS)) for turn in range(OFFS)]


def dot(left, right, contract):
    return lax.dot_general(
        left, right, ((contract[:1], contract[1:]), ((), ())), preferred_element_type=F32
    )


def nn(left, right):
    return dot(left, right, (1, 0))


def nt(left, right):
    return dot(left, right, (1, 1))


def tn(left, right):
    return dot(left, right, (0, 0))


def split_pair(cells):
    low = lax.broadcasted_iota(jnp.int32, cells.shape, 1) < HD
    zero = jnp.zeros_like(cells)
    return jnp.concatenate([jnp.where(low, cells, zero), jnp.where(low, zero, cells)], axis=0)


def lanes(pair):
    return slice(pair * 2 * HD, (pair + 1) * 2 * HD)


EDGE = REACH * BLK


def chunk(base, count, which):
    return pl.ds(base * 4 + which, count, stride=4)


def virtual_sums_kernel(
    k_ref, v_ref, vq_ref, vg_ref, out_ref, to_left_ref, to_right_ref, held, sem
):
    loads = [
        pltpu.make_async_copy(ref, held.at[which], sem.at[which])
        for which, ref in enumerate((k_ref, v_ref))
    ]
    for copy in loads:
        copy.start()
    copies = []
    for which in range(2):
        loads[which].wait()
        for start, ref in ((0, to_left_ref), (ROWS - EDGE, to_right_ref)):
            copies.append(
                pltpu.make_async_copy(
                    held.at[which, pl.ds(start, EDGE)], ref.at[which], sem.at[2 + len(copies)]
                )
            )
            copies[-1].start()
    for pair in range(PAIRS):
        sl = lanes(pair)
        keys, values = held[0, :, sl], held[1, :, sl]
        wq = split_pair(vq_ref[:, sl] * SCALE).astype(BF16)
        wg = split_pair(vg_ref[:, sl])
        scores = nt(keys, wq)
        top = jnp.max(scores, axis=0, keepdims=True)
        p = jnp.exp(scores - top)
        total = jnp.sum(p, axis=0, keepdims=True)
        gv = nt(values, wg)
        centre = jnp.sum(p * gv, axis=0, keepdims=True) / total
        rounded = p.astype(BF16)
        weighted = tn(rounded, values)
        first = tn((p * (gv - centre)).astype(BF16), keys)
        second = tn(rounded, keys)
        stats = jnp.concatenate(
            [top, total, centre, jnp.zeros((2 * VC - 3, 2 * VC), F32)], axis=0
        ).T
        for half in range(2):
            rows = slice(half * VC, (half + 1) * VC)
            part = slice(half * HD, (half + 1) * HD)
            at = (pair % 2) * 2 * VC + half * VC
            base = (pair // 2) * 2
            out_ref[chunk(at, VC, base), :] = jnp.concatenate(
                [weighted[rows, part], stats[rows, :HD]], axis=1
            )
            out_ref[chunk(at, VC, base + 1), :] = jnp.concatenate(
                [first[rows, part], second[rows, part]], axis=1
            )
    for copy in copies:
        copy.wait()


def wanted_row(requests, member):
    return pl.multiple_of((requests[member % OFFS][member] % NB) * BLK, BLK)


def pack_kernel(*refs):
    requests, owned, outs, sem = refs[:OFFS], refs[OFFS : OFFS + 2], refs[OFFS + 2 : -1], refs[-1]
    copies = []
    for member in range(FAR):
        turn, slot = member % OFFS, member // OFFS
        for which, ref in enumerate(owned):
            copies.append(
                pltpu.make_async_copy(
                    ref.at[pl.ds(wanted_row(requests, member), BLK)],
                    outs[turn].at[slot, which],
                    sem.at[len(copies)],
                )
            )
            copies[-1].start()
    for copy in copies:
        copy.wait()


def virtual_merge_kernel(parts_ref, sums_ref, vg_ref, out_ref):
    devices = parts_ref.shape[0] // 4
    me = lax.axis_index("nodes")
    lane = lax.broadcasted_iota(jnp.int32, (1, 128), 1)
    for n in range(2):
        out_ref[pl.ds(4 + n, devices, stride=6), :] = sums_ref[pl.ds(n, devices, stride=2), :]
    query = lax.broadcasted_iota(jnp.int32, vg_ref.shape, 0)
    grads = jnp.sum(jnp.where(query == me % VC, vg_ref[...].astype(F32), 0.0), axis=0, keepdims=True)
    for c in range(2):
        grad_row = jnp.zeros((1, HD), F32)
        for head in range(HEADS // 2):
            at = (c * (HEADS // 2) + head) * HD
            grad_row = jnp.where(me // VC == head, grads[:, at : at + HD], grad_row)
        one = parts_ref[chunk(0, devices, 2 * c), :]
        two = parts_ref[chunk(0, devices, 2 * c + 1), :]
        top, total, centre = (one[:, HD + n : HD + n + 1] for n in range(3))
        highest = jnp.max(top, axis=0, keepdims=True)
        scale = jnp.exp(top - highest)
        all_total = jnp.sum(scale * total, axis=0, keepdims=True)
        output = jnp.sum(scale * one[:, :HD], axis=0, keepdims=True) / all_total
        output = output.astype(BF16).astype(F32)
        vdelta = jnp.sum(grad_row * output, axis=1, keepdims=True)
        grad = jnp.sum(
            scale * (two[:, :HD] + (centre - vdelta) * two[:, HD:]), axis=0, keepdims=True
        )
        grad = grad * (SCALE / all_total)
        stats = jnp.where(lane == 0, highest, jnp.where(lane == 1, all_total, vdelta))
        result = jnp.concatenate([output, grad], axis=1)
        out_ref[pl.ds(2 * c, devices, stride=6), :] = jnp.broadcast_to(result, (devices, 128))
        out_ref[pl.ds(2 * c + 1, devices, stride=6), :] = jnp.broadcast_to(stats, (devices, 128))


def block_place(cols_ref, b, e):
    return pl.multiple_of((cols_ref[b, e] - cols_ref[0, 0] + REACH) * BLK, BLK)


def edges_kernel(
    cols_ref,
    bits_ref,
    q_ref,
    g_ref,
    k_ref,
    v_ref,
    left_ref,
    right_ref,
    vk_ref,
    vv_ref,
    far0,
    far1,
    far2,
    far3,
    far4,
    out_ref,
    ds_ref,
    p_ref,
    sums_ref,
    fg0,
    fg1,
    fg2,
    fg3,
    fg4,
    band,
    far,
    far_grads,
    cat,
    bias,
    virt_acc,
    sem,
    out_sem,
):
    fars = (far0, far1, far2, far3, far4)
    far_outs = (fg0, fg1, fg2, fg3, fg4)
    b = pl.program_id(0)

    @pl.when(b == 0)
    def start():
        arrivals = [
            pltpu.make_async_copy(fars[m % OFFS].at[m // OFFS], far.at[m], sem.at[m])
            for m in range(FAR)
        ]
        for copy in arrivals:
            copy.start()
        for which, own in enumerate((k_ref, v_ref)):
            band[which, 0:EDGE] = left_ref[which]
            band[which, EDGE : EDGE + ROWS] = own[...]
            band[which, EDGE + ROWS : 2 * EDGE + ROWS] = right_ref[which]
        cat[0, COLS:ALL] = vk_ref[...]
        cat[1, COLS:ALL] = vv_ref[...]
        bias[COLS:ALL] = jnp.zeros((VC, 2 * BLK), F32)
        virt_acc[...] = jnp.zeros(virt_acc.shape, F32)
        for copy in arrivals:
            copy.wait()

    row_lane = lax.broadcasted_iota(jnp.int32, (1, 2 * BLK), 1) % BLK
    col_row = lax.broadcasted_iota(jnp.int32, (BLK, 2 * BLK), 0)

    def pick(words, index):
        word = index // 32
        chosen = jnp.where(
            word == 0, words[0], jnp.where(word == 1, words[1], jnp.where(word == 2, words[2], words[3]))
        )
        return (jnp.right_shift(chosen, index % 32) & 1) > 0

    for e in range(LOC + EXP):
        at = slice(e * BLK, (e + 1) * BLK)
        for which in range(2):
            if e < LOC:
                cat[which, at] = band[which, pl.ds(block_place(cols_ref, b, e), BLK)]
            else:
                cat[which, at] = far[b * EXP + (e - LOC), which]
        words = [bits_ref[b, e, w] for w in range(8)]
        linked = pick(words[:4], row_lane) & pick(words[4:], col_row)
        bias[at] = jnp.where(linked, 0.0, MASKED)
    for pair in range(PAIRS):
        sl = lanes(pair)
        grad = g_ref[:, sl]
        wq = split_pair(q_ref[:, sl] * SCALE).astype(BF16)
        wg = split_pair(grad)
        keys, values = cat[0, :, sl], cat[1, :, sl]
        scores = nt(keys, wq) + bias[...]
        top = jnp.max(scores, axis=0, keepdims=True)
        w = jnp.exp(scores - top)
        total = jnp.sum(w, axis=0, keepdims=True)
        p = w * (1.0 / total)
        rounded = p.astype(BF16)
        p_ref[0, pair] = rounded[: LOC * BLK]
        mixed = tn(values, rounded)
        output = jnp.concatenate([mixed[:HD, :BLK], mixed[HD:, BLK:]], axis=0)
        output = output.astype(BF16).astype(F32)
        out_ref[:, sl] = output.T.astype(BF16)
        product = output * grad.astype(F32).T
        delta = jnp.concatenate(
            [
                jnp.sum(product[:HD], axis=0, keepdims=True),
                jnp.sum(product[HD:], axis=0, keepdims=True),
            ],
            axis=1,
        )
        ds = (p * (nt(values, wg) - delta)).astype(BF16)
        ds_ref[0, pair] = ds
        for which, grads in enumerate((nn(ds[LOC * BLK :], wq), nn(rounded[LOC * BLK :], wg))):
            for e in range(EXP):
                far_grads[b * EXP + e, which, :, sl] = grads[e * BLK : (e + 1) * BLK].astype(BF16)
            virt_acc[which * PAIRS + pair] += grads[EXP * BLK :]

    leaving = [
        pltpu.make_async_copy(far_grads.at[m], far_outs[m % OFFS].at[m // OFFS], out_sem.at[m])
        for m in range(FAR)
    ]
    for row in range(NB):

        @pl.when(b == row)
        def send():
            for e in range(EXP):
                leaving[row * EXP + e].start()

    @pl.when(b == NB - 1)
    def finish():
        for part in range(2 * PAIRS):
            sums_ref[part * VC : (part + 1) * VC] = virt_acc[part]
        for copy in leaving:
            copy.wait()


def gradients_kernel(
    cols_ref,
    q_ref,
    g_ref,
    ds_ref,
    p_ref,
    k_ref,
    left_ref,
    right_ref,
    vk_ref,
    far0,
    far1,
    far2,
    far3,
    far4,
    gq_ref,
    own_ref,
    to_left_ref,
    to_right_ref,
    band,
    far,
    cat,
    acc,
    sem,
):
    fars = (far0, far1, far2, far3, far4)
    b = pl.program_id(0)

    @pl.when(b == 0)
    def start():
        arrivals = [
            pltpu.make_async_copy(fars[m % OFFS].at[m // OFFS, 0], far.at[m], sem.at[m])
            for m in range(FAR)
        ]
        for copy in arrivals:
            copy.start()
        band[0:EDGE] = left_ref[0]
        band[EDGE : EDGE + ROWS] = k_ref[...]
        band[EDGE + ROWS : 2 * EDGE + ROWS] = right_ref[0]
        acc[...] = jnp.zeros(acc.shape, F32)
        cat[COLS:ALL] = vk_ref[...]
        for copy in arrivals:
            copy.wait()

    places = [block_place(cols_ref, b, e) for e in range(LOC)]
    for e in range(LOC + EXP):
        at = slice(e * BLK, (e + 1) * BLK)
        if e < LOC:
            cat[at] = band[pl.ds(places[e], BLK)]
        else:
            cat[at] = far[b * EXP + (e - LOC)]
    for pair in range(PAIRS):
        sl = lanes(pair)
        wq = split_pair(q_ref[:, sl] * SCALE).astype(BF16)
        wg = split_pair(g_ref[:, sl])
        ds = ds_ref[0, pair]
        mixed = tn(cat[:, sl], ds)
        grad_q = jnp.concatenate([mixed[:HD, :BLK], mixed[HD:, BLK:]], axis=0)
        gq_ref[:, sl] = (grad_q * SCALE).T.astype(BF16)
        for which, grads in enumerate((nn(ds[: LOC * BLK], wq), nn(p_ref[0, pair], wg))):
            for e in range(LOC):
                acc[which, pl.ds(places[e], BLK), sl] += grads[e * BLK : (e + 1) * BLK]

    @pl.when(b == NB - 1)
    def finish():
        for which in range(2):
            to_left_ref[which] = acc[which, 0:EDGE].astype(BF16)
            own_ref[which] = acc[which, EDGE : EDGE + ROWS]
            to_right_ref[which] = acc[which, EDGE + ROWS : 2 * EDGE + ROWS].astype(BF16)


def share_sum_kernel(parts_ref, out_ref):
    devices = parts_ref.shape[0] // 6
    for n in range(2):
        total = jnp.sum(parts_ref[pl.ds(4 + n, devices, stride=6), :], axis=0, keepdims=True)
        out_ref[pl.ds(n, devices, stride=2), :] = jnp.broadcast_to(total, (devices, 128))


def share_place_kernel(shares_ref, gvk_ref, gvv_ref):
    for which, out in enumerate((gvk_ref, gvv_ref)):
        for pair in range(PAIRS):
            at = (which * PAIRS + pair) * VC
            out[:, lanes(pair)] = shares_ref[at : at + VC, :].astype(BF16)


def collect_kernel(
    want0,
    want1,
    want2,
    want3,
    want4,
    k_ref,
    v_ref,
    vq_ref,
    vg_ref,
    all_ref,
    own_ref,
    from_left_ref,
    from_right_ref,
    far0,
    far1,
    far2,
    far3,
    far4,
    gk_ref,
    gv_ref,
    vout_ref,
    gvq_ref,
    acc,
):
    fars = (far0, far1, far2, far3, far4)
    for head in range(HEADS):
        cells = all_ref[pl.ds((head % 4) * VC * 6 + (head // 4) * 2, VC, stride=6), :]
        vout_ref[:, head * HD : (head + 1) * HD] = cells[:, :HD].astype(BF16)
        gvq_ref[:, head * HD : (head + 1) * HD] = cells[:, HD:].astype(BF16)
    for pair in range(PAIRS):
        sl = lanes(pair)
        stats = all_ref[pl.ds((pair % 2) * 2 * VC * 6 + (pair // 2) * 2 + 1, 2 * VC, stride=6), :].T
        top, total, vdelta = stats[0:1], stats[1:2], stats[2:3]
        wq = split_pair(vq_ref[:, sl] * SCALE).astype(BF16)
        wg = split_pair(vg_ref[:, sl])
        p = jnp.exp(nt(k_ref[:, sl], wq) - top) * (1.0 / total)
        da = p * (nt(v_ref[:, sl], wg) - vdelta)
        for which, grads in enumerate((nn(da.astype(BF16), wq), nn(p.astype(BF16), wg))):
            acc[which, 0:EDGE, sl] = (
                grads[0:EDGE] + own_ref[which, 0:EDGE, sl] + from_left_ref[which, :, sl].astype(F32)
            )
            acc[which, EDGE:ROWS, sl] = (
                grads[EDGE:] + own_ref[which, EDGE:ROWS, sl] + from_right_ref[which, :, sl].astype(F32)
            )
    for member in range(FAR):
        start = wanted_row((want0, want1, want2, want3, want4), member)
        for which in range(2):
            acc[which, pl.ds(start, BLK)] += fars[member % OFFS][member // OFFS, which].astype(F32)
    gk_ref[...] = acc[0].astype(BF16)
    gv_ref[...] = acc[1].astype(BF16)


def vmem(count):
    return [pl.BlockSpec(memory_space=pltpu.VMEM)] * count


def smem(count):
    return [pl.BlockSpec(memory_space=pltpu.SMEM)] * count


def anywhere(count):
    return [pl.BlockSpec(memory_space=pl.ANY)] * count


def by_block(*dims):
    return pl.BlockSpec(dims, lambda b: (b,) + (0,) * (len(dims) - 1))


def shape(dims, dtype):
    return jax.ShapeDtypeStruct(dims, dtype)


def call(kernel, name, ins, outs, out_specs, scratch=(), grid=(), flops=0, moved=0, limit=58):
    return pl.pallas_call(
        kernel,
        out_shape=outs,
        grid=grid,
        in_specs=ins,
        out_specs=out_specs,
        scratch_shapes=list(scratch),
        name=name,
        cost_estimate=pl.CostEstimate(flops=flops, bytes_accessed=moved, transcendentals=0),
        compiler_params=pltpu.CompilerParams(vmem_limit_bytes=limit * 2**20),
    )


def shift(cells, distance):
    count = lax.axis_size("nodes")
    return lax.ppermute(cells, "nodes", [(i, (i + distance) % count) for i in range(count)])


def exchange(cells):
    return lax.all_to_all(cells, "nodes", 0, 0, tiled=True)


def on_device(
    node_q,
    node_k,
    node_v,
    node_grad,
    local_cols,
    expander_cols,
    edge_bits,
    virt_q,
    virt_k,
    virt_v,
    virt_grad,
):
    devices = lax.axis_size("nodes")
    distances = [devices >> (turn + 1) for turn in range(OFFS)]

    flat = expander_cols.reshape(FAR)
    requests = [shift(flat, distance) for distance in distances]
    packed_shapes = [shape((count, 2, BLK, D), BF16) for count in COUNTS]
    packed = call(
        pack_kernel,
        "pack_wanted",
        smem(OFFS) + vmem(2),
        packed_shapes,
        anywhere(OFFS),
        [pltpu.SemaphoreType.DMA((2 * FAR,))],
        moved=3 * 2**20,
    )(*requests, node_k, node_v)
    far = [shift(cells, -distance) for cells, distance in zip(packed, distances)]

    parts, to_left, to_right = call(
        virtual_sums_kernel,
        "virtual_sums",
        anywhere(2) + vmem(2),
        [shape((devices * 4, 128), F32)] + [shape((2, EDGE, D), BF16)] * 2,
        vmem(1) + anywhere(2),
        [pltpu.VMEM((2, ROWS, D), BF16), pltpu.SemaphoreType.DMA((6,))],
        flops=2 * ROWS * VC * D * 5,
        moved=4 * 2**20,
    )(node_k, node_v, virt_q, virt_grad)
    to_left, to_right, *far[3:] = lax.optimization_barrier((to_left, to_right, *far[3:]))
    from_left = shift(to_right, 1)
    from_right = shift(to_left, -1)
    parts, _ = lax.optimization_barrier((parts, packed))
    parts = exchange(parts)

    node_output, ds, p, sums, *far_grads = call(
        edges_kernel,
        "edges",
        smem(2) + [by_block(BLK, D)] * 2 + vmem(6) + anywhere(OFFS),
        [
            shape((ROWS, D), BF16),
            shape((NB, PAIRS, ALL, 2 * BLK), BF16),
            shape((NB, PAIRS, LOC * BLK, 2 * BLK), BF16),
            shape((devices * 2, 2 * HD), F32),
        ]
        + packed_shapes,
        [
            by_block(BLK, D),
            by_block(1, PAIRS, ALL, 2 * BLK),
            by_block(1, PAIRS, LOC * BLK, 2 * BLK),
        ]
        + vmem(1)
        + anywhere(OFFS),
        [
            pltpu.VMEM((2, BAND * BLK, D), BF16),
            pltpu.VMEM((FAR, 2, BLK, D), BF16),
            pltpu.VMEM((FAR, 2, BLK, D), BF16),
            pltpu.VMEM((2, ALL, D), BF16),
            pltpu.VMEM((ALL, 2 * BLK), F32),
            pltpu.VMEM((2 * PAIRS, VC, 2 * HD), F32),
            pltpu.SemaphoreType.DMA((FAR,)),
            pltpu.SemaphoreType.DMA((FAR,)),
        ],
        grid=(NB,),
        flops=1,
        moved=1,
    )(
        local_cols,
        edge_bits,
        node_q,
        node_grad,
        node_k,
        node_v,
        from_left,
        from_right,
        virt_k,
        virt_v,
        *far,
    )
    returned = [shift(cells, distance) for cells, distance in zip(far_grads, distances)]

    grad_q, own, to_left, to_right = call(
        gradients_kernel,
        "gradients",
        smem(1)
        + [by_block(BLK, D)] * 2
        + [by_block(1, PAIRS, ALL, 2 * BLK), by_block(1, PAIRS, LOC * BLK, 2 * BLK)]
        + vmem(4)
        + anywhere(OFFS),
        [
            shape((ROWS, D), BF16),
            shape((2, ROWS, D), F32),
            shape((2, EDGE, D), BF16),
            shape((2, EDGE, D), BF16),
        ],
        [by_block(BLK, D)] + vmem(3),
        [
            pltpu.VMEM((BAND * BLK, D), BF16),
            pltpu.VMEM((FAR, BLK, D), BF16),
            pltpu.VMEM((ALL, D), BF16),
            pltpu.VMEM((2, BAND * BLK, D), F32),
            pltpu.SemaphoreType.DMA((FAR,)),
        ],
        grid=(NB,),
        flops=1,
        moved=1,
    )(
        local_cols,
        node_q,
        node_grad,
        ds,
        p,
        node_k,
        from_left,
        from_right,
        virt_k,
        *far,
    )
    to_left, to_right, *returned[3:] = lax.optimization_barrier((to_left, to_right, *returned[3:]))
    from_right_grads = shift(to_left, -1)
    from_left_grads = shift(to_right, 1)

    sums = exchange(
        call(
            virtual_merge_kernel,
            "virtual_merge",
            vmem(3),
            shape((devices * 6, 128), F32),
            pl.BlockSpec(memory_space=pltpu.VMEM),
            flops=1,
            moved=1,
        )(parts, sums, virt_grad)
    )
    shares = call(
        share_sum_kernel,
        "share_sum",
        vmem(1),
        shape((devices * 2, 128), F32),
        pl.BlockSpec(memory_space=pltpu.VMEM),
        flops=2**18,
        moved=2**19,
    )(sums)
    grad_vk, grad_vv = call(
        share_place_kernel,
        "share_place",
        vmem(1),
        [shape((VC, D), BF16)] * 2,
        vmem(2),
        flops=2**16,
        moved=2**19,
    )(exchange(shares))

    grad_k, grad_v, virtual_output, grad_vq = call(
        collect_kernel,
        "collect",
        smem(OFFS) + vmem(8 + OFFS),
        [shape((ROWS, D), BF16)] * 2 + [shape((VC, D), BF16)] * 2,
        vmem(4),
        [pltpu.VMEM((2, ROWS, D), F32)],
        flops=2 * ROWS * VC * D * 4,
        moved=7 * 2**20,
    )(
        *requests,
        node_k,
        node_v,
        virt_q,
        virt_grad,
        sums,
        own,
        from_left_grads,
        from_right_grads,
        *returned,
    )
    return node_output, virtual_output, grad_q, grad_k, grad_v, grad_vq, grad_vk, grad_vv


def solution(mesh):
    rows = P("nodes", None)
    return jax.shard_map(
        on_device,
        mesh=mesh,
        in_specs=(rows,) * 6 + (P("nodes", None, None),) + (P(),) * 4,
        out_specs=(rows, P(), rows, rows, rows, P(), P(), P()),
        check_vma=False,
    )
```

```python
import functools
import math

import jax
import jax.numpy as jnp
from jax import lax
from jax.experimental import pallas as pl
from jax.experimental.pallas import tpu as pltpu
from jax.sharding import PartitionSpec as P

HEADS = 8
HD = 64
BLK = 128
NB = 4
LOC = 4
EXP = 2
OFFS = 5
VC = 64
REACH = 2
D = HEADS * HD
ROWS = NB * BLK
PAIRS = HEADS // 2
FAR = NB * EXP
COLS = (LOC + EXP) * BLK
ALL = COLS + VC
BAND = NB + 2 * REACH
SCALE = 1.0 / math.sqrt(HD)
MASKED = -1e30
F32 = jnp.float32
BF16 = jnp.bfloat16
HALF = FAR // 2


def dot(left, right, contract):
    return lax.dot_general(
        left, right, ((contract[:1], contract[1:]), ((), ())), preferred_element_type=F32
    )


def nn(left, right):
    return dot(left, right, (1, 0))


def nt(left, right):
    return dot(left, right, (1, 1))


def tn(left, right):
    return dot(left, right, (0, 0))


def split_pair(cells):
    low = lax.broadcasted_iota(jnp.int32, cells.shape, 1) < HD
    zero = jnp.zeros_like(cells)
    return jnp.concatenate([jnp.where(low, cells, zero), jnp.where(low, zero, cells)], axis=0)


def lanes(pair):
    return slice(pair * 2 * HD, (pair + 1) * 2 * HD)


EDGE = REACH * BLK


def chunk(base, count, which):
    return pl.ds(base * 4 + which, count, stride=4)


def virtual_sums_kernel(
    k_ref, v_ref, vq_ref, vg_ref, out_ref, to_left_ref, to_right_ref, held, sem
):
    loads = [
        pltpu.make_async_copy(ref, held.at[which], sem.at[which])
        for which, ref in enumerate((k_ref, v_ref))
    ]
    for copy in loads:
        copy.start()
    copies = []
    for which in range(2):
        loads[which].wait()
        for start, ref in ((0, to_left_ref), (ROWS - EDGE, to_right_ref)):
            copies.append(
                pltpu.make_async_copy(
                    held.at[which, pl.ds(start, EDGE)], ref.at[which], sem.at[2 + len(copies)]
                )
            )
            copies[-1].start()
    for pair in range(PAIRS):
        sl = lanes(pair)
        keys, values = held[0, :, sl], held[1, :, sl]
        wq = split_pair(vq_ref[:, sl] * SCALE).astype(BF16)
        wg = split_pair(vg_ref[:, sl])
        scores = nt(keys, wq)
        top = jnp.max(scores, axis=0, keepdims=True)
        p = jnp.exp(scores - top)
        total = jnp.sum(p, axis=0, keepdims=True)
        gv = nt(values, wg)
        centre = jnp.sum(p * gv, axis=0, keepdims=True) / total
        rounded = p.astype(BF16)
        weighted = tn(rounded, values)
        first = tn((p * (gv - centre)).astype(BF16), keys)
        second = tn(rounded, keys)
        stats = jnp.concatenate(
            [top, total, centre, jnp.zeros((2 * VC - 3, 2 * VC), F32)], axis=0
        ).T
        for half in range(2):
            rows = slice(half * VC, (half + 1) * VC)
            part = slice(half * HD, (half + 1) * HD)
            at = (pair % 2) * 2 * VC + half * VC
            base = (pair // 2) * 2
            out_ref[chunk(at, VC, base), :] = jnp.concatenate(
                [weighted[rows, part], stats[rows, :HD]], axis=1
            )
            out_ref[chunk(at, VC, base + 1), :] = jnp.concatenate(
                [first[rows, part], second[rows, part]], axis=1
            )
    for copy in copies:
        copy.wait()


def wanted_row(requests, member):
    return pl.multiple_of((requests[member % OFFS][member] % NB) * BLK, BLK)


def pack_kernel(*refs):
    requests, owned, outs, sem = refs[:OFFS], refs[OFFS : OFFS + 2], refs[OFFS + 2 : -1], refs[-1]
    copies = []
    for member in range(FAR):
        for which, ref in enumerate(owned):
            copies.append(
                pltpu.make_async_copy(
                    ref.at[pl.ds(wanted_row(requests, member), BLK)],
                    outs[member].at[which],
                    sem.at[len(copies)],
                )
            )
            copies[-1].start()
    for copy in copies:
        copy.wait()


def virtual_merge_kernel(parts_ref, sums_a_ref, sums_b_ref, vg_ref, out_ref, results_ref):
    devices = parts_ref.shape[0] // 4
    me = lax.axis_index("nodes")
    lane = lax.broadcasted_iota(jnp.int32, (1, 128), 1)
    stats = jnp.zeros((1, 128), F32)
    results = []
    for n in range(2):
        at = pl.ds(n, devices, stride=2)
        out_ref[chunk(0, devices, 1 + n), :] = sums_a_ref[at, :] + sums_b_ref[at, :]
    query = lax.broadcasted_iota(jnp.int32, vg_ref.shape, 0)
    grads = jnp.sum(jnp.where(query == me % VC, vg_ref[...].astype(F32), 0.0), axis=0, keepdims=True)
    for c in range(2):
        grad_row = jnp.zeros((1, HD), F32)
        for head in range(HEADS // 2):
            at = (c * (HEADS // 2) + head) * HD
            grad_row = jnp.where(me // VC == head, grads[:, at : at + HD], grad_row)
        one = parts_ref[chunk(0, devices, 2 * c), :]
        two = parts_ref[chunk(0, devices, 2 * c + 1), :]
        top, total, centre = (one[:, HD + n : HD + n + 1] for n in range(3))
        highest = jnp.max(top, axis=0, keepdims=True)
        scale = jnp.exp(top - highest)
        all_total = jnp.sum(scale * total, axis=0, keepdims=True)
        output = jnp.sum(scale * one[:, :HD], axis=0, keepdims=True) / all_total
        output = output.astype(BF16).astype(F32)
        vdelta = jnp.sum(grad_row * output, axis=1, keepdims=True)
        grad = jnp.sum(
            scale * (two[:, :HD] + (centre - vdelta) * two[:, HD:]), axis=0, keepdims=True
        )
        grad = grad * (SCALE / all_total)
        for n, cell in enumerate((highest, all_total, vdelta)):
            stats = jnp.where(lane == c * HD + n, cell, stats)
        results.append(jnp.concatenate([output, grad], axis=1))
    out_ref[chunk(0, devices, 0), :] = jnp.broadcast_to(stats, (devices, 128))
    out_ref[chunk(0, devices, 3), :] = jnp.zeros((devices, 128), F32)
    results_ref[...] = jnp.concatenate([*results, jnp.zeros((6, 128), F32)], axis=0)


def block_place(cols_ref, b, e):
    return pl.multiple_of((cols_ref[b, e] - cols_ref[0, 0] + REACH) * BLK, BLK)


def edges_kernel(
    first_block,
    cols_ref,
    bits_ref,
    q_ref,
    g_ref,
    k_ref,
    v_ref,
    left_ref,
    right_ref,
    vk_ref,
    vv_ref,
    *rest,
):
    fars, rest = rest[:HALF], rest[-13 - HALF + 1 :]
    out_ref, ds_ref, p_ref, sums_ref = rest[:4]
    far_outs = rest[4 : 4 + HALF]
    band, far, far_grads, cat, bias, virt_acc, sem, out_sem = rest[4 + HALF :]
    step = pl.program_id(0)
    b = first_block + step

    @pl.when(step == 0)
    def start():
        arrivals = [
            pltpu.make_async_copy(fars[m], far.at[m], sem.at[m]) for m in range(HALF)
        ]
        for copy in arrivals:
            copy.start()
        for which, own in enumerate((k_ref, v_ref)):
            band[which, 0:EDGE] = left_ref[which]
            band[which, EDGE : EDGE + ROWS] = own[...]
            band[which, EDGE + ROWS : 2 * EDGE + ROWS] = right_ref[which]
        cat[0, COLS:ALL] = vk_ref[...]
        cat[1, COLS:ALL] = vv_ref[...]
        bias[COLS:ALL] = jnp.zeros((VC, 2 * BLK), F32)
        virt_acc[...] = jnp.zeros(virt_acc.shape, F32)
        for copy in arrivals:
            copy.wait()

    row_lane = lax.broadcasted_iota(jnp.int32, (1, 2 * BLK), 1) % BLK
    col_row = lax.broadcasted_iota(jnp.int32, (BLK, 2 * BLK), 0)

    def pick(words, index):
        word = index // 32
        chosen = jnp.where(
            word == 0, words[0], jnp.where(word == 1, words[1], jnp.where(word == 2, words[2], words[3]))
        )
        return (jnp.right_shift(chosen, index % 32) & 1) > 0

    for e in range(LOC + EXP):
        at = slice(e * BLK, (e + 1) * BLK)
        for which in range(2):
            if e < LOC:
                cat[which, at] = band[which, pl.ds(block_place(cols_ref, b, e), BLK)]
            else:
                cat[which, at] = far[step * EXP + (e - LOC), which]
        words = [bits_ref[b, e, w] for w in range(8)]
        linked = pick(words[:4], row_lane) & pick(words[4:], col_row)
        bias[at] = jnp.where(linked, 0.0, MASKED)
    for pair in range(PAIRS):
        sl = lanes(pair)
        grad = g_ref[:, sl]
        wq = split_pair(q_ref[:, sl] * SCALE).astype(BF16)
        wg = split_pair(grad)
        keys, values = cat[0, :, sl], cat[1, :, sl]
        scores = nt(keys, wq) + bias[...]
        top = jnp.max(scores, axis=0, keepdims=True)
        w = jnp.exp(scores - top)
        total = jnp.sum(w, axis=0, keepdims=True)
        p = w * (1.0 / total)
        rounded = p.astype(BF16)
        p_ref[0, pair] = rounded[: LOC * BLK]
        mixed = tn(values, rounded)
        output = jnp.concatenate([mixed[:HD, :BLK], mixed[HD:, BLK:]], axis=0)
        output = output.astype(BF16).astype(F32)
        out_ref[:, sl] = output.T.astype(BF16)
        product = output * grad.astype(F32).T
        delta = jnp.concatenate(
            [
                jnp.sum(product[:HD], axis=0, keepdims=True),
                jnp.sum(product[HD:], axis=0, keepdims=True),
            ],
            axis=1,
        )
        ds = (p * (nt(values, wg) - delta)).astype(BF16)
        ds_ref[0, pair] = ds
        for which, grads in enumerate((nn(ds[LOC * BLK :], wq), nn(rounded[LOC * BLK :], wg))):
            for e in range(EXP):
                far_grads[step * EXP + e, which, :, sl] = grads[e * BLK : (e + 1) * BLK].astype(BF16)
            virt_acc[which * PAIRS + pair] += grads[EXP * BLK :]

    leaving = [
        pltpu.make_async_copy(far_grads.at[m], far_outs[m], out_sem.at[m]) for m in range(HALF)
    ]
    for row in range(HALF // EXP):

        @pl.when(step == row)
        def send():
            for e in range(EXP):
                leaving[row * EXP + e].start()

    @pl.when(step == HALF // EXP - 1)
    def finish():
        for part in range(2 * PAIRS):
            sums_ref[part * VC : (part + 1) * VC] = virt_acc[part]
        for copy in leaving:
            copy.wait()


def gradients_kernel(
    cols_ref,
    q_ref,
    g_ref,
    ds_ref,
    p_ref,
    k_ref,
    left_ref,
    right_ref,
    vk_ref,
    *rest,
):
    fars = rest[:FAR]
    gq_ref, own_ref, to_left_ref, to_right_ref, band, far, cat, acc, sem = rest[FAR:]
    b = pl.program_id(0)

    @pl.when(b == 0)
    def start():
        arrivals = [
            pltpu.make_async_copy(fars[m].at[0], far.at[m], sem.at[m])
            for m in range(FAR)
        ]
        for copy in arrivals:
            copy.start()
        band[0:EDGE] = left_ref[0]
        band[EDGE : EDGE + ROWS] = k_ref[...]
        band[EDGE + ROWS : 2 * EDGE + ROWS] = right_ref[0]
        acc[...] = jnp.zeros(acc.shape, F32)
        cat[COLS:ALL] = vk_ref[...]
        for copy in arrivals:
            copy.wait()

    places = [block_place(cols_ref, b, e) for e in range(LOC)]
    for e in range(LOC + EXP):
        at = slice(e * BLK, (e + 1) * BLK)
        if e < LOC:
            cat[at] = band[pl.ds(places[e], BLK)]
        else:
            cat[at] = far[b * EXP + (e - LOC)]
    for pair in range(PAIRS):
        sl = lanes(pair)
        wq = split_pair(q_ref[:, sl] * SCALE).astype(BF16)
        wg = split_pair(g_ref[:, sl])
        ds = ds_ref[0, pair]
        mixed = tn(cat[:, sl], ds)
        grad_q = jnp.concatenate([mixed[:HD, :BLK], mixed[HD:, BLK:]], axis=0)
        gq_ref[:, sl] = (grad_q * SCALE).T.astype(BF16)
        for which, grads in enumerate((nn(ds[: LOC * BLK], wq), nn(p_ref[0, pair], wg))):
            for e in range(LOC):
                acc[which, pl.ds(places[e], BLK), sl] += grads[e * BLK : (e + 1) * BLK]

    @pl.when(b == NB - 1)
    def finish():
        for which in range(2):
            to_left_ref[which] = acc[which, 0:EDGE].astype(BF16)
            own_ref[which] = acc[which, EDGE : EDGE + ROWS]
            to_right_ref[which] = acc[which, EDGE + ROWS : 2 * EDGE + ROWS].astype(BF16)


def share_sum_kernel(parts_ref, results_ref, out_ref):
    devices = parts_ref.shape[0] // 4
    rows = [results_ref[0:2]]
    for n in range(2):
        rows.append(jnp.sum(parts_ref[chunk(0, devices, 1 + n), :], axis=0, keepdims=True))
    cells = jnp.concatenate(rows * 4, axis=0).astype(BF16)
    for at in range(0, out_ref.shape[0], 16):
        out_ref[at : at + 16] = cells


def share_place_kernel(shares_ref, vout_ref, gvq_ref, gvk_ref, gvv_ref, held, placed):
    held[...] = shares_ref[...].astype(F32)
    devices = shares_ref.shape[0] // 4
    for head in range(HEADS):
        cells = held[chunk((head % 4) * VC, VC, head // 4), :].astype(BF16)
        vout_ref[:, head * HD : (head + 1) * HD] = cells[:, :HD]
        gvq_ref[:, head * HD : (head + 1) * HD] = cells[:, HD:]
    for n in range(2):
        placed[pl.ds(n, devices, stride=2), :] = held[chunk(0, devices, 2 + n), :]
    for which, out in enumerate((gvk_ref, gvv_ref)):
        for pair in range(PAIRS):
            at = (which * PAIRS + pair) * VC
            out[:, lanes(pair)] = placed[at : at + VC, :].astype(BF16)


def collect_kernel(
    want0,
    want1,
    want2,
    want3,
    want4,
    k_ref,
    v_ref,
    vq_ref,
    vg_ref,
    all_ref,
    own_ref,
    from_left_ref,
    from_right_ref,
    *rest,
):
    fars = rest[:FAR]
    gk_ref, gv_ref, acc = rest[FAR:]
    for pair in range(PAIRS):
        sl = lanes(pair)
        stats = all_ref[chunk((pair % 2) * 2 * VC, 2 * VC, 0), :].T
        base = (pair // 2) * HD
        top, total, vdelta = (stats[base + n : base + n + 1] for n in range(3))
        wq = split_pair(vq_ref[:, sl] * SCALE).astype(BF16)
        wg = split_pair(vg_ref[:, sl])
        p = jnp.exp(nt(k_ref[:, sl], wq) - top) * (1.0 / total)
        da = p * (nt(v_ref[:, sl], wg) - vdelta)
        for which, grads in enumerate((nn(da.astype(BF16), wq), nn(p.astype(BF16), wg))):
            acc[which, 0:EDGE, sl] = (
                grads[0:EDGE] + own_ref[which, 0:EDGE, sl] + from_left_ref[which, :, sl].astype(F32)
            )
            acc[which, EDGE:ROWS, sl] = (
                grads[EDGE:] + own_ref[which, EDGE:ROWS, sl] + from_right_ref[which, :, sl].astype(F32)
            )
    for member in range(FAR):
        start = wanted_row((want0, want1, want2, want3, want4), member)
        for which in range(2):
            acc[which, pl.ds(start, BLK)] += fars[member][which].astype(F32)
    gk_ref[...] = acc[0].astype(BF16)
    gv_ref[...] = acc[1].astype(BF16)


def vmem(count):
    return [pl.BlockSpec(memory_space=pltpu.VMEM)] * count


def smem(count):
    return [pl.BlockSpec(memory_space=pltpu.SMEM)] * count


def anywhere(count):
    return [pl.BlockSpec(memory_space=pl.ANY)] * count


def by_block(*dims, first=0):
    return pl.BlockSpec(dims, lambda b: (b + first,) + (0,) * (len(dims) - 1))


def shape(dims, dtype):
    return jax.ShapeDtypeStruct(dims, dtype)


def call(kernel, name, ins, outs, out_specs, scratch=(), grid=(), flops=0, moved=0, limit=58, aliases=()):
    return pl.pallas_call(
        kernel,
        out_shape=outs,
        grid=grid,
        in_specs=ins,
        out_specs=out_specs,
        scratch_shapes=list(scratch),
        name=name,
        input_output_aliases=dict(aliases),
        cost_estimate=pl.CostEstimate(flops=flops, bytes_accessed=moved, transcendentals=0),
        compiler_params=pltpu.CompilerParams(vmem_limit_bytes=limit * 2**20),
    )


def shift(cells, distance):
    count = lax.axis_size("nodes")
    return lax.ppermute(cells, "nodes", [(i, (i + distance) % count) for i in range(count)])


def exchange(cells):
    return lax.all_to_all(cells, "nodes", 0, 0, tiled=True)


def on_device(
    node_q,
    node_k,
    node_v,
    node_grad,
    local_cols,
    expander_cols,
    edge_bits,
    virt_q,
    virt_k,
    virt_v,
    virt_grad,
):
    devices = lax.axis_size("nodes")
    distances = [devices >> (turn + 1) for turn in range(OFFS)]
    steps = [distances[member % OFFS] for member in range(FAR)]

    flat = expander_cols.reshape(FAR)
    requests = [shift(flat, distance) for distance in distances]
    parts, to_left, to_right = call(
        virtual_sums_kernel,
        "virtual_sums",
        anywhere(2) + vmem(2),
        [shape((devices * 4, 128), F32)] + [shape((2, EDGE, D), BF16)] * 2,
        vmem(1) + anywhere(2),
        [pltpu.VMEM((2, ROWS, D), BF16), pltpu.SemaphoreType.DMA((6,))],
        flops=1,
        moved=1,
    )(node_k, node_v, virt_q, virt_grad)
    from_left = shift(to_right, 1)
    from_right = shift(to_left, -1)
    parts = exchange(parts)
    requests[0], from_left, from_right = lax.optimization_barrier(
        (requests[0], from_left, from_right)
    )
    one_block = shape((2, BLK, D), BF16)
    packed = call(
        pack_kernel,
        "pack_wanted",
        smem(OFFS) + vmem(2),
        [one_block] * FAR,
        anywhere(FAR),
        [pltpu.SemaphoreType.DMA((2 * FAR,))],
        flops=1,
        moved=1,
    )(*requests, node_k, node_v)
    far = [shift(cells, -step) for cells, step in zip(packed, steps)]

    edge_shapes = [
        shape((ROWS, D), BF16),
        shape((NB, PAIRS, ALL, 2 * BLK), BF16),
        shape((NB, PAIRS, LOC * BLK, 2 * BLK), BF16),
    ]
    earlier, sums, far_grads = [], [], []
    for half in range(2):
        first = half * (NB // 2)
        blocks = [
            by_block(BLK, D, first=first),
            by_block(1, PAIRS, ALL, 2 * BLK, first=first),
            by_block(1, PAIRS, LOC * BLK, 2 * BLK, first=first),
        ]
        outs = call(
            functools.partial(edges_kernel, first),
            "edges_first" if half == 0 else "edges_second",
            smem(2) + [blocks[0]] * 2 + vmem(6) + anywhere(HALF + len(earlier)),
            edge_shapes + [shape((devices * 2, 2 * HD), F32)] + [one_block] * HALF,
            blocks + vmem(1) + anywhere(HALF),
            [
                pltpu.VMEM((2, BAND * BLK, D), BF16),
                pltpu.VMEM((HALF, 2, BLK, D), BF16),
                pltpu.VMEM((HALF, 2, BLK, D), BF16),
                pltpu.VMEM((2, ALL, D), BF16),
                pltpu.VMEM((ALL, 2 * BLK), F32),
                pltpu.VMEM((2 * PAIRS, VC, 2 * HD), F32),
                pltpu.SemaphoreType.DMA((HALF,)),
                pltpu.SemaphoreType.DMA((HALF,)),
            ],
            grid=(NB // 2,),
            flops=1,
            moved=1,
            aliases=[(10 + HALF + n, n) for n in range(len(earlier))],
        )(
            local_cols,
            edge_bits,
            node_q,
            node_grad,
            node_k,
            node_v,
            from_left,
            from_right,
            virt_k,
            virt_v,
            *far[half * HALF : (half + 1) * HALF],
            *earlier,
        )
        earlier = outs[:3]
        sums.append(outs[3])
        far_grads.append(outs[4:])
    node_output, ds, p = earlier
    returned = [shift(cells, step) for cells, step in zip(far_grads[0], steps)]
    returned += [shift(cells, step) for cells, step in zip(far_grads[1], steps[HALF:])]

    grad_q, own, to_left, to_right = call(
        gradients_kernel,
        "gradients",
        smem(1)
        + [by_block(BLK, D)] * 2
        + [by_block(1, PAIRS, ALL, 2 * BLK), by_block(1, PAIRS, LOC * BLK, 2 * BLK)]
        + vmem(4)
        + anywhere(FAR),
        [
            shape((ROWS, D), BF16),
            shape((2, ROWS, D), F32),
            shape((2, EDGE, D), BF16),
            shape((2, EDGE, D), BF16),
        ],
        [by_block(BLK, D)] + vmem(3),
        [
            pltpu.VMEM((BAND * BLK, D), BF16),
            pltpu.VMEM((FAR, BLK, D), BF16),
            pltpu.VMEM((ALL, D), BF16),
            pltpu.VMEM((2, BAND * BLK, D), F32),
            pltpu.SemaphoreType.DMA((FAR,)),
        ],
        grid=(NB,),
        flops=1,
        moved=1,
    )(
        local_cols,
        node_q,
        node_grad,
        ds,
        p,
        node_k,
        from_left,
        from_right,
        virt_k,
        *far,
    )
    to_left, to_right, returned[HALF:] = lax.optimization_barrier(
        (to_left, to_right, returned[HALF:])
    )
    from_right_grads = shift(to_left, -1)
    from_left_grads = shift(to_right, 1)

    sums[1], returned[:HALF] = lax.optimization_barrier((sums[1], returned[:HALF]))
    merged, results = call(
        virtual_merge_kernel,
        "virtual_merge",
        vmem(4),
        [shape((devices * 4, 128), F32), shape((8, 128), F32)],
        vmem(2),
        flops=1,
        moved=1,
    )(parts, *sums, virt_grad)
    merged = exchange(merged)
    shares = call(
        share_sum_kernel,
        "share_sum",
        vmem(2),
        shape((devices * 4, 128), BF16),
        pl.BlockSpec(memory_space=pltpu.VMEM),
        flops=1,
        moved=1,
    )(merged, results)
    virtual_output, grad_vq, grad_vk, grad_vv = call(
        share_place_kernel,
        "share_place",
        vmem(1),
        [shape((VC, D), BF16)] * 4,
        vmem(4),
        [pltpu.VMEM((devices * 4, 128), F32), pltpu.VMEM((devices * 2, 128), F32)],
        flops=1,
        moved=1,
    )(exchange(shares))

    grad_k, grad_v = call(
        collect_kernel,
        "collect",
        smem(OFFS) + vmem(8 + FAR),
        [shape((ROWS, D), BF16)] * 2,
        vmem(2),
        [pltpu.VMEM((2, ROWS, D), F32)],
        flops=2 * ROWS * VC * D * 4,
        moved=7 * 2**20,
    )(
        *requests,
        node_k,
        node_v,
        virt_q,
        virt_grad,
        merged,
        own,
        from_left_grads,
        from_right_grads,
        *returned,
    )
    return node_output, virtual_output, grad_q, grad_k, grad_v, grad_vq, grad_vk, grad_vv


def solution(mesh):
    rows = P("nodes", None)
    return jax.shard_map(
        on_device,
        mesh=mesh,
        in_specs=(rows,) * 6 + (P("nodes", None, None),) + (P(),) * 4,
        out_specs=(rows, P(), rows, rows, rows, P(), P(), P()),
        check_vma=False,
    )
```

```python
import functools
import math

import jax
import jax.numpy as jnp
from jax import lax
from jax.experimental import pallas as pl
from jax.experimental.pallas import tpu as pltpu
from jax.sharding import PartitionSpec as P

HEADS = 8
HD = 64
BLK = 128
NB = 4
LOC = 4
EXP = 2
OFFS = 5
VC = 64
REACH = 2
D = HEADS * HD
ROWS = NB * BLK
PAIRS = HEADS // 2
FAR = NB * EXP
COLS = (LOC + EXP) * BLK
ALL = COLS + VC
BAND = NB + 2 * REACH
SCALE = 1.0 / math.sqrt(HD)
MASKED = -1e30
F32 = jnp.float32
BF16 = jnp.bfloat16
HALF = FAR // 2


def dot(left, right, contract):
    return lax.dot_general(
        left, right, ((contract[:1], contract[1:]), ((), ())), preferred_element_type=F32
    )


def nn(left, right):
    return dot(left, right, (1, 0))


def nt(left, right):
    return dot(left, right, (1, 1))


def tn(left, right):
    return dot(left, right, (0, 0))


def split_pair(cells):
    low = lax.broadcasted_iota(jnp.int32, cells.shape, 1) < HD
    zero = jnp.zeros_like(cells)
    return jnp.concatenate([jnp.where(low, cells, zero), jnp.where(low, zero, cells)], axis=0)


def lanes(pair):
    return slice(pair * 2 * HD, (pair + 1) * 2 * HD)


EDGE = REACH * BLK


def chunk(base, count, which):
    return pl.ds(base * 4 + which, count, stride=4)


def virtual_sums_kernel(
    k_ref, v_ref, vq_ref, vg_ref, out_ref, to_left_ref, to_right_ref, held, sem
):
    loads = [
        pltpu.make_async_copy(ref, held.at[which], sem.at[which])
        for which, ref in enumerate((k_ref, v_ref))
    ]
    for copy in loads:
        copy.start()
    copies = []
    for which in range(2):
        loads[which].wait()
        for start, ref in ((0, to_left_ref), (ROWS - EDGE, to_right_ref)):
            copies.append(
                pltpu.make_async_copy(
                    held.at[which, pl.ds(start, EDGE)], ref.at[which], sem.at[2 + len(copies)]
                )
            )
            copies[-1].start()
    for pair in range(PAIRS):
        sl = lanes(pair)
        keys, values = held[0, :, sl], held[1, :, sl]
        wq = split_pair(vq_ref[:, sl] * SCALE).astype(BF16)
        wg = split_pair(vg_ref[:, sl])
        scores = nt(keys, wq)
        top = jnp.max(scores, axis=0, keepdims=True)
        p = jnp.exp(scores - top)
        total = jnp.sum(p, axis=0, keepdims=True)
        gv = nt(values, wg)
        centre = jnp.sum(p * gv, axis=0, keepdims=True) / total
        rounded = p.astype(BF16)
        weighted = tn(rounded, values)
        first = tn((p * (gv - centre)).astype(BF16), keys)
        second = tn(rounded, keys)
        stats = jnp.concatenate(
            [top, total, centre, jnp.zeros((2 * VC - 3, 2 * VC), F32)], axis=0
        ).T
        for half in range(2):
            rows = slice(half * VC, (half + 1) * VC)
            part = slice(half * HD, (half + 1) * HD)
            at = (pair % 2) * 2 * VC + half * VC
            base = (pair // 2) * 2
            out_ref[chunk(at, VC, base), :] = jnp.concatenate(
                [weighted[rows, part], stats[rows, :HD]], axis=1
            )
            out_ref[chunk(at, VC, base + 1), :] = jnp.concatenate(
                [first[rows, part], second[rows, part]], axis=1
            )
    for copy in copies:
        copy.wait()


def wanted_row(requests, member):
    return pl.multiple_of((requests[member % OFFS][member] % NB) * BLK, BLK)


def pack_kernel(*refs):
    requests, owned, outs, sem = refs[:OFFS], refs[OFFS : OFFS + 2], refs[OFFS + 2 : -1], refs[-1]
    copies = []
    for member in range(FAR):
        for which, ref in enumerate(owned):
            copies.append(
                pltpu.make_async_copy(
                    ref.at[pl.ds(wanted_row(requests, member), BLK)],
                    outs[member].at[which],
                    sem.at[len(copies)],
                )
            )
            copies[-1].start()
    for copy in copies:
        copy.wait()


def virtual_merge_kernel(parts_ref, sums_a_ref, sums_b_ref, vg_ref, out_ref, results_ref):
    devices = parts_ref.shape[0] // 4
    me = lax.axis_index("nodes")
    lane = lax.broadcasted_iota(jnp.int32, (1, 128), 1)
    stats = jnp.zeros((1, 128), F32)
    results = []
    for n in range(2):
        at = pl.ds(n, devices, stride=2)
        out_ref[chunk(0, devices, 1 + n), :] = sums_a_ref[at, :] + sums_b_ref[at, :]
    query = lax.broadcasted_iota(jnp.int32, vg_ref.shape, 0)
    grads = jnp.sum(jnp.where(query == me % VC, vg_ref[...].astype(F32), 0.0), axis=0, keepdims=True)
    for c in range(2):
        grad_row = jnp.zeros((1, HD), F32)
        for head in range(HEADS // 2):
            at = (c * (HEADS // 2) + head) * HD
            grad_row = jnp.where(me // VC == head, grads[:, at : at + HD], grad_row)
        one = parts_ref[chunk(0, devices, 2 * c), :]
        two = parts_ref[chunk(0, devices, 2 * c + 1), :]
        top, total, centre = (one[:, HD + n : HD + n + 1] for n in range(3))
        highest = jnp.max(top, axis=0, keepdims=True)
        scale = jnp.exp(top - highest)
        all_total = jnp.sum(scale * total, axis=0, keepdims=True)
        output = jnp.sum(scale * one[:, :HD], axis=0, keepdims=True) / all_total
        output = output.astype(BF16).astype(F32)
        vdelta = jnp.sum(grad_row * output, axis=1, keepdims=True)
        grad = jnp.sum(
            scale * (two[:, :HD] + (centre - vdelta) * two[:, HD:]), axis=0, keepdims=True
        )
        grad = grad * (SCALE / all_total)
        for n, cell in enumerate((highest, all_total, vdelta)):
            stats = jnp.where(lane == c * HD + n, cell, stats)
        results.append(jnp.concatenate([output, grad], axis=1))
    out_ref[chunk(0, devices, 0), :] = jnp.broadcast_to(stats, (devices, 128))
    out_ref[chunk(0, devices, 3), :] = jnp.zeros((devices, 128), F32)
    results_ref[...] = jnp.concatenate([*results, jnp.zeros((6, 128), F32)], axis=0)


def block_place(cols_ref, b, e):
    return pl.multiple_of((cols_ref[b, e] - cols_ref[0, 0] + REACH) * BLK, BLK)


def edges_kernel(
    first_block,
    cols_ref,
    bits_ref,
    q_ref,
    g_ref,
    k_ref,
    v_ref,
    left_ref,
    right_ref,
    vk_ref,
    vv_ref,
    *rest,
):
    fars, rest = rest[:HALF], rest[-13 - HALF + 1 :]
    out_ref, ds_ref, p_ref, sums_ref = rest[:4]
    far_outs = rest[4 : 4 + HALF]
    band, far, far_grads, cat, bias, virt_acc, sem, out_sem = rest[4 + HALF :]
    step = pl.program_id(0)
    b = first_block + step

    @pl.when(step == 0)
    def start():
        arrivals = [
            pltpu.make_async_copy(fars[m], far.at[m], sem.at[m]) for m in range(HALF)
        ]
        for copy in arrivals:
            copy.start()
        for which, own in enumerate((k_ref, v_ref)):
            band[which, 0:EDGE] = left_ref[which]
            band[which, EDGE : EDGE + ROWS] = own[...]
            band[which, EDGE + ROWS : 2 * EDGE + ROWS] = right_ref[which]
        cat[0, COLS:ALL] = vk_ref[...]
        cat[1, COLS:ALL] = vv_ref[...]
        bias[COLS:ALL] = jnp.zeros((VC, 2 * BLK), F32)
        virt_acc[...] = jnp.zeros(virt_acc.shape, F32)
        for copy in arrivals:
            copy.wait()

    row_lane = lax.broadcasted_iota(jnp.int32, (1, 2 * BLK), 1) % BLK
    col_row = lax.broadcasted_iota(jnp.int32, (BLK, 2 * BLK), 0)

    def pick(words, index):
        word = index // 32
        chosen = jnp.where(
            word == 0, words[0], jnp.where(word == 1, words[1], jnp.where(word == 2, words[2], words[3]))
        )
        return (jnp.right_shift(chosen, index % 32) & 1) > 0

    for e in range(LOC + EXP):
        at = slice(e * BLK, (e + 1) * BLK)
        for which in range(2):
            if e < LOC:
                cat[which, at] = band[which, pl.ds(block_place(cols_ref, b, e), BLK)]
            else:
                cat[which, at] = far[step * EXP + (e - LOC), which]
        words = [bits_ref[b, e, w] for w in range(8)]
        linked = pick(words[:4], row_lane) & pick(words[4:], col_row)
        bias[at] = jnp.where(linked, 0.0, MASKED)
    for pair in range(PAIRS):
        sl = lanes(pair)
        grad = g_ref[:, sl]
        wq = split_pair(q_ref[:, sl] * SCALE).astype(BF16)
        wg = split_pair(grad)
        keys, values = cat[0, :, sl], cat[1, :, sl]
        scores = nt(keys, wq) + bias[...]
        top = jnp.max(scores, axis=0, keepdims=True)
        w = jnp.exp(scores - top)
        total = jnp.sum(w, axis=0, keepdims=True)
        p = w * (1.0 / total)
        rounded = p.astype(BF16)
        p_ref[0, pair] = rounded[: LOC * BLK]
        mixed = tn(values, rounded)
        output = jnp.concatenate([mixed[:HD, :BLK], mixed[HD:, BLK:]], axis=0)
        output = output.astype(BF16).astype(F32)
        out_ref[:, sl] = output.T.astype(BF16)
        product = output * grad.astype(F32).T
        delta = jnp.concatenate(
            [
                jnp.sum(product[:HD], axis=0, keepdims=True),
                jnp.sum(product[HD:], axis=0, keepdims=True),
            ],
            axis=1,
        )
        ds = (p * (nt(values, wg) - delta)).astype(BF16)
        ds_ref[0, pair] = ds
        for which, grads in enumerate((nn(ds[LOC * BLK :], wq), nn(rounded[LOC * BLK :], wg))):
            for e in range(EXP):
                far_grads[step * EXP + e, which, :, sl] = grads[e * BLK : (e + 1) * BLK].astype(BF16)
            virt_acc[which * PAIRS + pair] += grads[EXP * BLK :]

    leaving = [
        pltpu.make_async_copy(far_grads.at[m], far_outs[m], out_sem.at[m]) for m in range(HALF)
    ]
    for row in range(HALF // EXP):

        @pl.when(step == row)
        def send():
            for e in range(EXP):
                leaving[row * EXP + e].start()

    @pl.when(step == HALF // EXP - 1)
    def finish():
        for part in range(2 * PAIRS):
            sums_ref[part * VC : (part + 1) * VC] = virt_acc[part]
        for copy in leaving:
            copy.wait()


def gradients_kernel(
    cols_ref,
    q_ref,
    g_ref,
    ds_ref,
    p_ref,
    k_ref,
    left_ref,
    right_ref,
    vk_ref,
    *rest,
):
    fars = rest[:FAR]
    gq_ref, own_ref, to_left_ref, to_right_ref, band, far, cat, acc, sem = rest[FAR:]
    b = pl.program_id(0)

    @pl.when(b == 0)
    def start():
        arrivals = [
            pltpu.make_async_copy(fars[m].at[0], far.at[m], sem.at[m])
            for m in range(FAR)
        ]
        for copy in arrivals:
            copy.start()
        band[0:EDGE] = left_ref[0]
        band[EDGE : EDGE + ROWS] = k_ref[...]
        band[EDGE + ROWS : 2 * EDGE + ROWS] = right_ref[0]
        acc[...] = jnp.zeros(acc.shape, F32)
        cat[COLS:ALL] = vk_ref[...]
        for copy in arrivals:
            copy.wait()

    places = [block_place(cols_ref, b, e) for e in range(LOC)]
    for e in range(LOC + EXP):
        at = slice(e * BLK, (e + 1) * BLK)
        if e < LOC:
            cat[at] = band[pl.ds(places[e], BLK)]
        else:
            cat[at] = far[b * EXP + (e - LOC)]
    for pair in range(PAIRS):
        sl = lanes(pair)
        wq = split_pair(q_ref[:, sl] * SCALE).astype(BF16)
        wg = split_pair(g_ref[:, sl])
        ds = ds_ref[0, pair]
        mixed = tn(cat[:, sl], ds)
        grad_q = jnp.concatenate([mixed[:HD, :BLK], mixed[HD:, BLK:]], axis=0)
        gq_ref[:, sl] = (grad_q * SCALE).T.astype(BF16)
        for which, grads in enumerate((nn(ds[: LOC * BLK], wq), nn(p_ref[0, pair], wg))):
            for e in range(LOC):
                acc[which, pl.ds(places[e], BLK), sl] += grads[e * BLK : (e + 1) * BLK]

    @pl.when(b == NB - 1)
    def finish():
        for which in range(2):
            to_left_ref[which] = acc[which, 0:EDGE].astype(BF16)
            own_ref[which] = acc[which, EDGE : EDGE + ROWS]
            to_right_ref[which] = acc[which, EDGE + ROWS : 2 * EDGE + ROWS].astype(BF16)


def share_sum_kernel(parts_ref, results_ref, out_ref):
    devices = parts_ref.shape[0] // 4
    rows = [results_ref[0:2]]
    for n in range(2):
        rows.append(jnp.sum(parts_ref[chunk(0, devices, 1 + n), :], axis=0, keepdims=True))
    cells = jnp.concatenate(rows * 4, axis=0).astype(BF16)
    for at in range(0, out_ref.shape[0], 16):
        out_ref[at : at + 16] = cells


def share_place_kernel(shares_ref, vout_ref, gvq_ref, gvk_ref, gvv_ref, held, placed):
    held[...] = shares_ref[...].astype(F32)
    devices = shares_ref.shape[0] // 4
    for head in range(HEADS):
        cells = held[chunk((head % 4) * VC, VC, head // 4), :].astype(BF16)
        vout_ref[:, head * HD : (head + 1) * HD] = cells[:, :HD]
        gvq_ref[:, head * HD : (head + 1) * HD] = cells[:, HD:]
    for n in range(2):
        placed[pl.ds(n, devices, stride=2), :] = held[chunk(0, devices, 2 + n), :]
    for which, out in enumerate((gvk_ref, gvv_ref)):
        for pair in range(PAIRS):
            at = (which * PAIRS + pair) * VC
            out[:, lanes(pair)] = placed[at : at + VC, :].astype(BF16)


def collect_kernel(
    want0,
    want1,
    want2,
    want3,
    want4,
    k_ref,
    v_ref,
    vq_ref,
    vg_ref,
    all_ref,
    own_ref,
    from_left_ref,
    from_right_ref,
    *rest,
):
    fars = rest[:FAR]
    gk_ref, gv_ref, acc = rest[FAR:]
    for pair in range(PAIRS):
        sl = lanes(pair)
        stats = all_ref[chunk((pair % 2) * 2 * VC, 2 * VC, 0), :].T
        base = (pair // 2) * HD
        top, total, vdelta = (stats[base + n : base + n + 1] for n in range(3))
        wq = split_pair(vq_ref[:, sl] * SCALE).astype(BF16)
        wg = split_pair(vg_ref[:, sl])
        p = jnp.exp(nt(k_ref[:, sl], wq) - top) * (1.0 / total)
        da = p * (nt(v_ref[:, sl], wg) - vdelta)
        for which, grads in enumerate((nn(da.astype(BF16), wq), nn(p.astype(BF16), wg))):
            acc[which, 0:EDGE, sl] = (
                grads[0:EDGE] + own_ref[which, 0:EDGE, sl] + from_left_ref[which, :, sl].astype(F32)
            )
            acc[which, EDGE:ROWS, sl] = (
                grads[EDGE:] + own_ref[which, EDGE:ROWS, sl] + from_right_ref[which, :, sl].astype(F32)
            )
    for member in range(FAR):
        start = wanted_row((want0, want1, want2, want3, want4), member)
        for which in range(2):
            acc[which, pl.ds(start, BLK)] += fars[member][which].astype(F32)
    gk_ref[...] = acc[0].astype(BF16)
    gv_ref[...] = acc[1].astype(BF16)


def vmem(count):
    return [pl.BlockSpec(memory_space=pltpu.VMEM)] * count


def smem(count):
    return [pl.BlockSpec(memory_space=pltpu.SMEM)] * count


def anywhere(count):
    return [pl.BlockSpec(memory_space=pl.ANY)] * count


def by_block(*dims, first=0):
    return pl.BlockSpec(dims, lambda b: (b + first,) + (0,) * (len(dims) - 1))


def shape(dims, dtype):
    return jax.ShapeDtypeStruct(dims, dtype)


def call(kernel, name, ins, outs, out_specs, scratch=(), grid=(), flops=0, moved=0, limit=58, aliases=()):
    return pl.pallas_call(
        kernel,
        out_shape=outs,
        grid=grid,
        in_specs=ins,
        out_specs=out_specs,
        scratch_shapes=list(scratch),
        name=name,
        input_output_aliases=dict(aliases),
        cost_estimate=pl.CostEstimate(flops=flops, bytes_accessed=moved, transcendentals=0),
        compiler_params=pltpu.CompilerParams(vmem_limit_bytes=limit * 2**20),
    )


def shift(cells, distance):
    count = lax.axis_size("nodes")
    return lax.ppermute(cells, "nodes", [(i, (i + distance) % count) for i in range(count)])


def exchange(cells):
    return lax.all_to_all(cells, "nodes", 0, 0, tiled=True)


def on_device(
    node_q,
    node_k,
    node_v,
    node_grad,
    local_cols,
    expander_cols,
    edge_bits,
    virt_q,
    virt_k,
    virt_v,
    virt_grad,
):
    devices = lax.axis_size("nodes")
    distances = [devices >> (turn + 1) for turn in range(OFFS)]
    steps = [distances[member % OFFS] for member in range(FAR)]

    flat = expander_cols.reshape(FAR)
    requests = [shift(flat, distance) for distance in distances]
    parts, to_left, to_right = call(
        virtual_sums_kernel,
        "virtual_sums",
        anywhere(2) + vmem(2),
        [shape((devices * 4, 128), F32)] + [shape((2, EDGE, D), BF16)] * 2,
        vmem(1) + anywhere(2),
        [pltpu.VMEM((2, ROWS, D), BF16), pltpu.SemaphoreType.DMA((6,))],
        flops=1,
        moved=1,
    )(node_k, node_v, virt_q, virt_grad)
    from_left = shift(to_right, 1)
    from_right = shift(to_left, -1)
    requests[0], from_left, from_right = lax.optimization_barrier(
        (requests[0], from_left, from_right)
    )
    one_block = shape((2, BLK, D), BF16)
    packed = call(
        pack_kernel,
        "pack_wanted",
        smem(OFFS) + vmem(2),
        [one_block] * FAR,
        anywhere(FAR),
        [pltpu.SemaphoreType.DMA((2 * FAR,))],
        flops=1,
        moved=1,
    )(*requests, node_k, node_v)
    far = [shift(cells, -step) for cells, step in zip(packed, steps)]
    parts, far[:HALF] = lax.optimization_barrier((parts, far[:HALF]))
    parts = exchange(parts)

    edge_shapes = [
        shape((ROWS, D), BF16),
        shape((NB, PAIRS, ALL, 2 * BLK), BF16),
        shape((NB, PAIRS, LOC * BLK, 2 * BLK), BF16),
    ]
    earlier, sums, far_grads = [], [], []
    for half in range(2):
        first = half * (NB // 2)
        blocks = [
            by_block(BLK, D, first=first),
            by_block(1, PAIRS, ALL, 2 * BLK, first=first),
            by_block(1, PAIRS, LOC * BLK, 2 * BLK, first=first),
        ]
        outs = call(
            functools.partial(edges_kernel, first),
            "edges_first" if half == 0 else "edges_second",
            smem(2) + [blocks[0]] * 2 + vmem(6) + anywhere(HALF + len(earlier)),
            edge_shapes + [shape((devices * 2, 2 * HD), F32)] + [one_block] * HALF,
            blocks + vmem(1) + anywhere(HALF),
            [
                pltpu.VMEM((2, BAND * BLK, D), BF16),
                pltpu.VMEM((HALF, 2, BLK, D), BF16),
                pltpu.VMEM((HALF, 2, BLK, D), BF16),
                pltpu.VMEM((2, ALL, D), BF16),
                pltpu.VMEM((ALL, 2 * BLK), F32),
                pltpu.VMEM((2 * PAIRS, VC, 2 * HD), F32),
                pltpu.SemaphoreType.DMA((HALF,)),
                pltpu.SemaphoreType.DMA((HALF,)),
            ],
            grid=(NB // 2,),
            flops=1,
            moved=1,
            aliases=[(10 + HALF + n, n) for n in range(len(earlier))],
        )(
            local_cols,
            edge_bits,
            node_q,
            node_grad,
            node_k,
            node_v,
            from_left,
            from_right,
            virt_k,
            virt_v,
            *far[half * HALF : (half + 1) * HALF],
            *earlier,
        )
        earlier = outs[:3]
        sums.append(outs[3])
        far_grads.append(outs[4:])
    node_output, ds, p = earlier
    returned = [shift(cells, step) for cells, step in zip(far_grads[0], steps)]
    returned += [shift(cells, step) for cells, step in zip(far_grads[1], steps[HALF:])]

    grad_q, own, to_left, to_right = call(
        gradients_kernel,
        "gradients",
        smem(1)
        + [by_block(BLK, D)] * 2
        + [by_block(1, PAIRS, ALL, 2 * BLK), by_block(1, PAIRS, LOC * BLK, 2 * BLK)]
        + vmem(4)
        + anywhere(FAR),
        [
            shape((ROWS, D), BF16),
            shape((2, ROWS, D), F32),
            shape((2, EDGE, D), BF16),
            shape((2, EDGE, D), BF16),
        ],
        [by_block(BLK, D)] + vmem(3),
        [
            pltpu.VMEM((BAND * BLK, D), BF16),
            pltpu.VMEM((FAR, BLK, D), BF16),
            pltpu.VMEM((ALL, D), BF16),
            pltpu.VMEM((2, BAND * BLK, D), F32),
            pltpu.SemaphoreType.DMA((FAR,)),
        ],
        grid=(NB,),
        flops=1,
        moved=1,
    )(
        local_cols,
        node_q,
        node_grad,
        ds,
        p,
        node_k,
        from_left,
        from_right,
        virt_k,
        *far,
    )
    to_left, to_right, returned[HALF:] = lax.optimization_barrier(
        (to_left, to_right, returned[HALF:])
    )
    from_right_grads = shift(to_left, -1)
    from_left_grads = shift(to_right, 1)

    sums[1], returned[:HALF] = lax.optimization_barrier((sums[1], returned[:HALF]))
    merged, results = call(
        virtual_merge_kernel,
        "virtual_merge",
        vmem(4),
        [shape((devices * 4, 128), F32), shape((8, 128), F32)],
        vmem(2),
        flops=1,
        moved=1,
    )(parts, *sums, virt_grad)
    merged = exchange(merged)
    shares = call(
        share_sum_kernel,
        "share_sum",
        vmem(2),
        shape((devices * 4, 128), BF16),
        pl.BlockSpec(memory_space=pltpu.VMEM),
        flops=1,
        moved=1,
    )(merged, results)
    virtual_output, grad_vq, grad_vk, grad_vv = call(
        share_place_kernel,
        "share_place",
        vmem(1),
        [shape((VC, D), BF16)] * 4,
        vmem(4),
        [pltpu.VMEM((devices * 4, 128), F32), pltpu.VMEM((devices * 2, 128), F32)],
        flops=1,
        moved=1,
    )(exchange(shares))

    grad_k, grad_v = call(
        collect_kernel,
        "collect",
        smem(OFFS) + vmem(8 + FAR),
        [shape((ROWS, D), BF16)] * 2,
        vmem(2),
        [pltpu.VMEM((2, ROWS, D), F32)],
        flops=2 * ROWS * VC * D * 4,
        moved=7 * 2**20,
    )(
        *requests,
        node_k,
        node_v,
        virt_q,
        virt_grad,
        merged,
        own,
        from_left_grads,
        from_right_grads,
        *returned,
    )
    return node_output, virtual_output, grad_q, grad_k, grad_v, grad_vq, grad_vk, grad_vv


def solution(mesh):
    rows = P("nodes", None)
    return jax.shard_map(
        on_device,
        mesh=mesh,
        in_specs=(rows,) * 6 + (P("nodes", None, None),) + (P(),) * 4,
        out_specs=(rows, P(), rows, rows, rows, P(), P(), P()),
        check_vma=False,
    )
```

```python
import functools
import math

import jax
import jax.numpy as jnp
from jax import lax
from jax.experimental import pallas as pl
from jax.experimental.pallas import tpu as pltpu
from jax.sharding import PartitionSpec as P

HEADS = 8
HD = 64
BLK = 128
NB = 4
LOC = 4
EXP = 2
OFFS = 5
VC = 64
REACH = 2
D = HEADS * HD
ROWS = NB * BLK
PAIRS = HEADS // 2
FAR = NB * EXP
COLS = (LOC + EXP) * BLK
ALL = COLS + VC
BAND = NB + 2 * REACH
SCALE = 1.0 / math.sqrt(HD)
MASKED = -1e30
F32 = jnp.float32
BF16 = jnp.bfloat16
HALF = FAR // 2


def dot(left, right, contract):
    return lax.dot_general(
        left, right, ((contract[:1], contract[1:]), ((), ())), preferred_element_type=F32
    )


def nn(left, right):
    return dot(left, right, (1, 0))


def nt(left, right):
    return dot(left, right, (1, 1))


def tn(left, right):
    return dot(left, right, (0, 0))


def split_pair(cells):
    low = lax.broadcasted_iota(jnp.int32, cells.shape, 1) < HD
    zero = jnp.zeros_like(cells)
    return jnp.concatenate([jnp.where(low, cells, zero), jnp.where(low, zero, cells)], axis=0)


def lanes(pair):
    return slice(pair * 2 * HD, (pair + 1) * 2 * HD)


EDGE = REACH * BLK


def chunk(base, count, which):
    return pl.ds(base * 4 + which, count, stride=4)


def virtual_sums_kernel(
    k_ref, v_ref, vq_ref, vg_ref, out_ref, to_left_ref, to_right_ref, held, sem
):
    loads = [
        pltpu.make_async_copy(ref, held.at[which], sem.at[which])
        for which, ref in enumerate((k_ref, v_ref))
    ]
    for copy in loads:
        copy.start()
    copies = []
    for which in range(2):
        loads[which].wait()
        for start, ref in ((0, to_left_ref), (ROWS - EDGE, to_right_ref)):
            copies.append(
                pltpu.make_async_copy(
                    held.at[which, pl.ds(start, EDGE)], ref.at[which], sem.at[2 + len(copies)]
                )
            )
            copies[-1].start()
    for pair in range(PAIRS):
        sl = lanes(pair)
        keys, values = held[0, :, sl], held[1, :, sl]
        wq = split_pair(vq_ref[:, sl] * SCALE).astype(BF16)
        wg = split_pair(vg_ref[:, sl])
        scores = nt(keys, wq)
        top = jnp.max(scores, axis=0, keepdims=True)
        p = jnp.exp(scores - top)
        total = jnp.sum(p, axis=0, keepdims=True)
        gv = nt(values, wg)
        centre = jnp.sum(p * gv, axis=0, keepdims=True) / total
        rounded = p.astype(BF16)
        weighted = tn(rounded, values)
        first = tn((p * (gv - centre)).astype(BF16), keys)
        second = tn(rounded, keys)
        stats = jnp.concatenate(
            [top, total, centre, jnp.zeros((2 * VC - 3, 2 * VC), F32)], axis=0
        ).T
        for half in range(2):
            rows = slice(half * VC, (half + 1) * VC)
            part = slice(half * HD, (half + 1) * HD)
            at = (pair % 2) * 2 * VC + half * VC
            base = (pair // 2) * 2
            out_ref[chunk(at, VC, base), :] = jnp.concatenate(
                [weighted[rows, part], stats[rows, :HD]], axis=1
            )
            out_ref[chunk(at, VC, base + 1), :] = jnp.concatenate(
                [first[rows, part], second[rows, part]], axis=1
            )
    for copy in copies:
        copy.wait()


def wanted_row(requests, member):
    return pl.multiple_of((requests[member % OFFS][member] % NB) * BLK, BLK)


def pack_kernel(*refs):
    requests, owned, outs, sem = refs[:OFFS], refs[OFFS : OFFS + 2], refs[OFFS + 2 : -1], refs[-1]
    copies = []
    for member in range(FAR):
        for which, ref in enumerate(owned):
            copies.append(
                pltpu.make_async_copy(
                    ref.at[pl.ds(wanted_row(requests, member), BLK)],
                    outs[member].at[which],
                    sem.at[len(copies)],
                )
            )
            copies[-1].start()
    for copy in copies:
        copy.wait()


def virtual_merge_kernel(parts_ref, sums_a_ref, sums_b_ref, vg_ref, out_ref, results_ref):
    devices = parts_ref.shape[0] // 4
    me = lax.axis_index("nodes")
    lane = lax.broadcasted_iota(jnp.int32, (1, 128), 1)
    stats = jnp.zeros((1, 128), F32)
    results = []
    for n in range(2):
        at = pl.ds(n, devices, stride=2)
        out_ref[chunk(0, devices, 1 + n), :] = sums_a_ref[at, :] + sums_b_ref[at, :]
    query = lax.broadcasted_iota(jnp.int32, vg_ref.shape, 0)
    grads = jnp.sum(jnp.where(query == me % VC, vg_ref[...].astype(F32), 0.0), axis=0, keepdims=True)
    for c in range(2):
        grad_row = jnp.zeros((1, HD), F32)
        for head in range(HEADS // 2):
            at = (c * (HEADS // 2) + head) * HD
            grad_row = jnp.where(me // VC == head, grads[:, at : at + HD], grad_row)
        one = parts_ref[chunk(0, devices, 2 * c), :]
        two = parts_ref[chunk(0, devices, 2 * c + 1), :]
        top, total, centre = (one[:, HD + n : HD + n + 1] for n in range(3))
        highest = jnp.max(top, axis=0, keepdims=True)
        scale = jnp.exp(top - highest)
        all_total = jnp.sum(scale * total, axis=0, keepdims=True)
        output = jnp.sum(scale * one[:, :HD], axis=0, keepdims=True) / all_total
        output = output.astype(BF16).astype(F32)
        vdelta = jnp.sum(grad_row * output, axis=1, keepdims=True)
        grad = jnp.sum(
            scale * (two[:, :HD] + (centre - vdelta) * two[:, HD:]), axis=0, keepdims=True
        )
        grad = grad * (SCALE / all_total)
        for n, cell in enumerate((highest, all_total, vdelta)):
            stats = jnp.where(lane == c * HD + n, cell, stats)
        results.append(jnp.concatenate([output, grad], axis=1))
    out_ref[chunk(0, devices, 0), :] = jnp.broadcast_to(stats, (devices, 128))
    out_ref[chunk(0, devices, 3), :] = jnp.zeros((devices, 128), F32)
    results_ref[...] = jnp.concatenate([*results, jnp.zeros((6, 128), F32)], axis=0)


def block_place(cols_ref, b, e):
    return pl.multiple_of((cols_ref[b, e] - cols_ref[0, 0] + REACH) * BLK, BLK)


def edges_kernel(
    first_block,
    cols_ref,
    bits_ref,
    q_ref,
    g_ref,
    k_ref,
    v_ref,
    left_ref,
    right_ref,
    vk_ref,
    vv_ref,
    *rest,
):
    fars, rest = rest[:HALF], rest[-13 - HALF + 1 :]
    out_ref, ds_ref, p_ref, sums_ref = rest[:4]
    far_outs = rest[4 : 4 + HALF]
    band, far, far_grads, cat, bias, virt_acc, sem, out_sem = rest[4 + HALF :]
    step = pl.program_id(0)
    b = first_block + step

    @pl.when(step == 0)
    def start():
        arrivals = [
            pltpu.make_async_copy(fars[m], far.at[m], sem.at[m]) for m in range(HALF)
        ]
        for copy in arrivals:
            copy.start()
        for which, own in enumerate((k_ref, v_ref)):
            band[which, 0:EDGE] = left_ref[which]
            band[which, EDGE : EDGE + ROWS] = own[...]
            band[which, EDGE + ROWS : 2 * EDGE + ROWS] = right_ref[which]
        cat[0, COLS:ALL] = vk_ref[...]
        cat[1, COLS:ALL] = vv_ref[...]
        bias[COLS:ALL] = jnp.zeros((VC, 2 * BLK), F32)
        virt_acc[...] = jnp.zeros(virt_acc.shape, F32)
        for copy in arrivals:
            copy.wait()

    row_lane = lax.broadcasted_iota(jnp.int32, (1, 2 * BLK), 1) % BLK
    col_row = lax.broadcasted_iota(jnp.int32, (BLK, 2 * BLK), 0)

    def pick(words, index):
        word = index // 32
        chosen = jnp.where(
            word == 0, words[0], jnp.where(word == 1, words[1], jnp.where(word == 2, words[2], words[3]))
        )
        return (jnp.right_shift(chosen, index % 32) & 1) > 0

    for e in range(LOC + EXP):
        at = slice(e * BLK, (e + 1) * BLK)
        for which in range(2):
            if e < LOC:
                cat[which, at] = band[which, pl.ds(block_place(cols_ref, b, e), BLK)]
            else:
                cat[which, at] = far[step * EXP + (e - LOC), which]
        words = [bits_ref[b, e, w] for w in range(8)]
        linked = pick(words[:4], row_lane) & pick(words[4:], col_row)
        bias[at] = jnp.where(linked, 0.0, MASKED)
    for pair in range(PAIRS):
        sl = lanes(pair)
        grad = g_ref[:, sl]
        wq = split_pair(q_ref[:, sl] * SCALE).astype(BF16)
        wg = split_pair(grad)
        keys, values = cat[0, :, sl], cat[1, :, sl]
        scores = nt(keys, wq) + bias[...]
        top = jnp.max(scores, axis=0, keepdims=True)
        w = jnp.exp(scores - top)
        total = jnp.sum(w, axis=0, keepdims=True)
        p = w * (1.0 / total)
        rounded = p.astype(BF16)
        p_ref[0, pair] = rounded[: LOC * BLK]
        mixed = tn(values, rounded)
        output = jnp.concatenate([mixed[:HD, :BLK], mixed[HD:, BLK:]], axis=0)
        output = output.astype(BF16).astype(F32)
        out_ref[:, sl] = output.T.astype(BF16)
        product = output * grad.astype(F32).T
        delta = jnp.concatenate(
            [
                jnp.sum(product[:HD], axis=0, keepdims=True),
                jnp.sum(product[HD:], axis=0, keepdims=True),
            ],
            axis=1,
        )
        ds = (p * (nt(values, wg) - delta)).astype(BF16)
        ds_ref[0, pair] = ds
        for which, grads in enumerate((nn(ds[LOC * BLK :], wq), nn(rounded[LOC * BLK :], wg))):
            for e in range(EXP):
                far_grads[step * EXP + e, which, :, sl] = grads[e * BLK : (e + 1) * BLK].astype(BF16)
            virt_acc[which * PAIRS + pair] += grads[EXP * BLK :]

    leaving = [
        pltpu.make_async_copy(far_grads.at[m], far_outs[m], out_sem.at[m]) for m in range(HALF)
    ]
    for row in range(HALF // EXP):

        @pl.when(step == row)
        def send():
            for e in range(EXP):
                leaving[row * EXP + e].start()

    @pl.when(step == HALF // EXP - 1)
    def finish():
        for part in range(2 * PAIRS):
            sums_ref[part * VC : (part + 1) * VC] = virt_acc[part]
        for copy in leaving:
            copy.wait()


def gradients_kernel(
    cols_ref,
    q_ref,
    g_ref,
    ds_ref,
    p_ref,
    k_ref,
    left_ref,
    right_ref,
    vk_ref,
    *rest,
):
    fars = rest[:FAR]
    gq_ref, own_ref, to_left_ref, to_right_ref, band, far, cat, acc, sem = rest[FAR:]
    b = pl.program_id(0)

    @pl.when(b == 0)
    def start():
        arrivals = [
            pltpu.make_async_copy(fars[m].at[0], far.at[m], sem.at[m])
            for m in range(FAR)
        ]
        for copy in arrivals:
            copy.start()
        band[0:EDGE] = left_ref[0]
        band[EDGE : EDGE + ROWS] = k_ref[...]
        band[EDGE + ROWS : 2 * EDGE + ROWS] = right_ref[0]
        acc[...] = jnp.zeros(acc.shape, F32)
        cat[COLS:ALL] = vk_ref[...]
        for copy in arrivals:
            copy.wait()

    places = [block_place(cols_ref, b, e) for e in range(LOC)]
    for e in range(LOC + EXP):
        at = slice(e * BLK, (e + 1) * BLK)
        if e < LOC:
            cat[at] = band[pl.ds(places[e], BLK)]
        else:
            cat[at] = far[b * EXP + (e - LOC)]
    for pair in range(PAIRS):
        sl = lanes(pair)
        wq = split_pair(q_ref[:, sl] * SCALE).astype(BF16)
        wg = split_pair(g_ref[:, sl])
        ds = ds_ref[0, pair]
        mixed = tn(cat[:, sl], ds)
        grad_q = jnp.concatenate([mixed[:HD, :BLK], mixed[HD:, BLK:]], axis=0)
        gq_ref[:, sl] = (grad_q * SCALE).T.astype(BF16)
        for which, grads in enumerate((nn(ds[: LOC * BLK], wq), nn(p_ref[0, pair], wg))):
            for e in range(LOC):
                acc[which, pl.ds(places[e], BLK), sl] += grads[e * BLK : (e + 1) * BLK]

    @pl.when(b == NB - 1)
    def finish():
        for which in range(2):
            to_left_ref[which] = acc[which, 0:EDGE].astype(BF16)
            own_ref[which] = acc[which, EDGE : EDGE + ROWS]
            to_right_ref[which] = acc[which, EDGE + ROWS : 2 * EDGE + ROWS].astype(BF16)


def share_sum_kernel(parts_ref, results_ref, out_ref):
    devices = parts_ref.shape[0] // 4
    rows = [results_ref[0:2]]
    for n in range(2):
        rows.append(jnp.sum(parts_ref[chunk(0, devices, 1 + n), :], axis=0, keepdims=True))
    cells = jnp.concatenate(rows * 4, axis=0).astype(BF16)
    for at in range(0, out_ref.shape[0], 16):
        out_ref[at : at + 16] = cells


def share_place_kernel(shares_ref, vout_ref, gvq_ref, gvk_ref, gvv_ref, held, placed):
    held[...] = shares_ref[...].astype(F32)
    devices = shares_ref.shape[0] // 4
    for head in range(HEADS):
        cells = held[chunk((head % 4) * VC, VC, head // 4), :].astype(BF16)
        vout_ref[:, head * HD : (head + 1) * HD] = cells[:, :HD]
        gvq_ref[:, head * HD : (head + 1) * HD] = cells[:, HD:]
    for n in range(2):
        placed[pl.ds(n, devices, stride=2), :] = held[chunk(0, devices, 2 + n), :]
    for which, out in enumerate((gvk_ref, gvv_ref)):
        for pair in range(PAIRS):
            at = (which * PAIRS + pair) * VC
            out[:, lanes(pair)] = placed[at : at + VC, :].astype(BF16)


def collect_kernel(
    want0,
    want1,
    want2,
    want3,
    want4,
    k_ref,
    v_ref,
    vq_ref,
    vg_ref,
    all_ref,
    own_ref,
    from_left_ref,
    from_right_ref,
    *rest,
):
    fars = rest[:FAR]
    gk_ref, gv_ref, acc = rest[FAR:]
    for pair in range(PAIRS):
        sl = lanes(pair)
        stats = all_ref[chunk((pair % 2) * 2 * VC, 2 * VC, 0), :].T
        base = (pair // 2) * HD
        top, total, vdelta = (stats[base + n : base + n + 1] for n in range(3))
        wq = split_pair(vq_ref[:, sl] * SCALE).astype(BF16)
        wg = split_pair(vg_ref[:, sl])
        p = jnp.exp(nt(k_ref[:, sl], wq) - top) * (1.0 / total)
        da = p * (nt(v_ref[:, sl], wg) - vdelta)
        for which, grads in enumerate((nn(da.astype(BF16), wq), nn(p.astype(BF16), wg))):
            acc[which, 0:EDGE, sl] = (
                grads[0:EDGE] + own_ref[which, 0:EDGE, sl] + from_left_ref[which, :, sl].astype(F32)
            )
            acc[which, EDGE:ROWS, sl] = (
                grads[EDGE:] + own_ref[which, EDGE:ROWS, sl] + from_right_ref[which, :, sl].astype(F32)
            )
    for member in range(FAR):
        start = wanted_row((want0, want1, want2, want3, want4), member)
        for which in range(2):
            acc[which, pl.ds(start, BLK)] += fars[member][which].astype(F32)
    gk_ref[...] = acc[0].astype(BF16)
    gv_ref[...] = acc[1].astype(BF16)


def vmem(count):
    return [pl.BlockSpec(memory_space=pltpu.VMEM)] * count


def smem(count):
    return [pl.BlockSpec(memory_space=pltpu.SMEM)] * count


def anywhere(count):
    return [pl.BlockSpec(memory_space=pl.ANY)] * count


def by_block(*dims, first=0):
    return pl.BlockSpec(dims, lambda b: (b + first,) + (0,) * (len(dims) - 1))


def shape(dims, dtype):
    return jax.ShapeDtypeStruct(dims, dtype)


def call(kernel, name, ins, outs, out_specs, scratch=(), grid=(), flops=0, moved=0, limit=58, aliases=()):
    return pl.pallas_call(
        kernel,
        out_shape=outs,
        grid=grid,
        in_specs=ins,
        out_specs=out_specs,
        scratch_shapes=list(scratch),
        name=name,
        input_output_aliases=dict(aliases),
        cost_estimate=pl.CostEstimate(flops=flops, bytes_accessed=moved, transcendentals=0),
        compiler_params=pltpu.CompilerParams(vmem_limit_bytes=limit * 2**20),
    )


def shift(cells, distance):
    count = lax.axis_size("nodes")
    return lax.ppermute(cells, "nodes", [(i, (i + distance) % count) for i in range(count)])


def exchange(cells):
    return lax.all_to_all(cells, "nodes", 0, 0, tiled=True)


def on_device(
    node_q,
    node_k,
    node_v,
    node_grad,
    local_cols,
    expander_cols,
    edge_bits,
    virt_q,
    virt_k,
    virt_v,
    virt_grad,
):
    devices = lax.axis_size("nodes")
    distances = [devices >> (turn + 1) for turn in range(OFFS)]
    steps = [distances[member % OFFS] for member in range(FAR)]

    flat = expander_cols.reshape(FAR)
    requests = [shift(flat, distance) for distance in distances]
    parts, to_left, to_right = call(
        virtual_sums_kernel,
        "virtual_sums",
        anywhere(2) + vmem(2),
        [shape((devices * 4, 128), F32)] + [shape((2, EDGE, D), BF16)] * 2,
        vmem(1) + anywhere(2),
        [pltpu.VMEM((2, ROWS, D), BF16), pltpu.SemaphoreType.DMA((6,))],
        flops=1,
        moved=1,
    )(node_k, node_v, virt_q, virt_grad)
    from_left = shift(to_right, 1)
    from_right = shift(to_left, -1)
    requests[0], from_left, from_right = lax.optimization_barrier(
        (requests[0], from_left, from_right)
    )
    one_block = shape((2, BLK, D), BF16)
    packed = call(
        pack_kernel,
        "pack_wanted",
        smem(OFFS) + vmem(2),
        [one_block] * FAR,
        anywhere(FAR),
        [pltpu.SemaphoreType.DMA((2 * FAR,))],
        flops=1,
        moved=1,
    )(*requests, node_k, node_v)
    far = [shift(cells, -step) for cells, step in zip(packed, steps)]

    edge_shapes = [
        shape((ROWS, D), BF16),
        shape((NB, PAIRS, ALL, 2 * BLK), BF16),
        shape((NB, PAIRS, LOC * BLK, 2 * BLK), BF16),
    ]
    earlier, sums, far_grads = [], [], []
    for half in range(2):
        first = half * (NB // 2)
        blocks = [
            by_block(BLK, D, first=first),
            by_block(1, PAIRS, ALL, 2 * BLK, first=first),
            by_block(1, PAIRS, LOC * BLK, 2 * BLK, first=first),
        ]
        outs = call(
            functools.partial(edges_kernel, first),
            "edges_first" if half == 0 else "edges_second",
            smem(2) + [blocks[0]] * 2 + vmem(6) + anywhere(HALF + len(earlier)),
            edge_shapes + [shape((devices * 2, 2 * HD), F32)] + [one_block] * HALF,
            blocks + vmem(1) + anywhere(HALF),
            [
                pltpu.VMEM((2, BAND * BLK, D), BF16),
                pltpu.VMEM((HALF, 2, BLK, D), BF16),
                pltpu.VMEM((HALF, 2, BLK, D), BF16),
                pltpu.VMEM((2, ALL, D), BF16),
                pltpu.VMEM((ALL, 2 * BLK), F32),
                pltpu.VMEM((2 * PAIRS, VC, 2 * HD), F32),
                pltpu.SemaphoreType.DMA((HALF,)),
                pltpu.SemaphoreType.DMA((HALF,)),
            ],
            grid=(NB // 2,),
            flops=1,
            moved=1,
            aliases=[(10 + HALF + n, n) for n in range(len(earlier))],
        )(
            local_cols,
            edge_bits,
            node_q,
            node_grad,
            node_k,
            node_v,
            from_left,
            from_right,
            virt_k,
            virt_v,
            *far[half * HALF : (half + 1) * HALF],
            *earlier,
        )
        earlier = outs[:3]
        sums.append(outs[3])
        far_grads.append(outs[4:])
        if half == 0:
            parts, sums[0], far[HALF:] = lax.optimization_barrier((parts, sums[0], far[HALF:]))
            parts = exchange(parts)
    node_output, ds, p = earlier
    returned = [shift(cells, step) for cells, step in zip(far_grads[0], steps)]
    returned += [shift(cells, step) for cells, step in zip(far_grads[1], steps[HALF:])]

    grad_q, own, to_left, to_right = call(
        gradients_kernel,
        "gradients",
        smem(1)
        + [by_block(BLK, D)] * 2
        + [by_block(1, PAIRS, ALL, 2 * BLK), by_block(1, PAIRS, LOC * BLK, 2 * BLK)]
        + vmem(4)
        + anywhere(FAR),
        [
            shape((ROWS, D), BF16),
            shape((2, ROWS, D), F32),
            shape((2, EDGE, D), BF16),
            shape((2, EDGE, D), BF16),
        ],
        [by_block(BLK, D)] + vmem(3),
        [
            pltpu.VMEM((BAND * BLK, D), BF16),
            pltpu.VMEM((FAR, BLK, D), BF16),
            pltpu.VMEM((ALL, D), BF16),
            pltpu.VMEM((2, BAND * BLK, D), F32),
            pltpu.SemaphoreType.DMA((FAR,)),
        ],
        grid=(NB,),
        flops=1,
        moved=1,
    )(
        local_cols,
        node_q,
        node_grad,
        ds,
        p,
        node_k,
        from_left,
        from_right,
        virt_k,
        *far,
    )
    to_left, to_right, returned[HALF + 1 :] = lax.optimization_barrier(
        (to_left, to_right, returned[HALF + 1 :])
    )
    from_right_grads = shift(to_left, -1)
    from_left_grads = shift(to_right, 1)

    sums[1], returned[:HALF] = lax.optimization_barrier((sums[1], returned[:HALF]))
    merged, results = call(
        virtual_merge_kernel,
        "virtual_merge",
        vmem(4),
        [shape((devices * 4, 128), F32), shape((8, 128), F32)],
        vmem(2),
        flops=1,
        moved=1,
    )(parts, *sums, virt_grad)
    merged = exchange(merged)
    shares = call(
        share_sum_kernel,
        "share_sum",
        vmem(2),
        shape((devices * 4, 128), BF16),
        pl.BlockSpec(memory_space=pltpu.VMEM),
        flops=1,
        moved=1,
    )(merged, results)
    virtual_output, grad_vq, grad_vk, grad_vv = call(
        share_place_kernel,
        "share_place",
        vmem(1),
        [shape((VC, D), BF16)] * 4,
        vmem(4),
        [pltpu.VMEM((devices * 4, 128), F32), pltpu.VMEM((devices * 2, 128), F32)],
        flops=1,
        moved=1,
    )(exchange(shares))

    grad_k, grad_v = call(
        collect_kernel,
        "collect",
        smem(OFFS) + vmem(8 + FAR),
        [shape((ROWS, D), BF16)] * 2,
        vmem(2),
        [pltpu.VMEM((2, ROWS, D), F32)],
        flops=2 * ROWS * VC * D * 4,
        moved=7 * 2**20,
    )(
        *requests,
        node_k,
        node_v,
        virt_q,
        virt_grad,
        merged,
        own,
        from_left_grads,
        from_right_grads,
        *returned,
    )
    return node_output, virtual_output, grad_q, grad_k, grad_v, grad_vq, grad_vk, grad_vv


def solution(mesh):
    rows = P("nodes", None)
    return jax.shard_map(
        on_device,
        mesh=mesh,
        in_specs=(rows,) * 6 + (P("nodes", None, None),) + (P(),) * 4,
        out_specs=(rows, P(), rows, rows, rows, P(), P(), P()),
        check_vma=False,
    )
```

```python
import functools
import math

import jax
import jax.numpy as jnp
from jax import lax
from jax.experimental import pallas as pl
from jax.experimental.pallas import tpu as pltpu
from jax.sharding import PartitionSpec as P

HEADS = 8
HD = 64
BLK = 128
NB = 4
LOC = 4
EXP = 2
OFFS = 5
VC = 64
REACH = 2
D = HEADS * HD
ROWS = NB * BLK
PAIRS = HEADS // 2
FAR = NB * EXP
COLS = (LOC + EXP) * BLK
ALL = COLS + VC
BAND = NB + 2 * REACH
SCALE = 1.0 / math.sqrt(HD)
MASKED = -1e30
F32 = jnp.float32
BF16 = jnp.bfloat16
HALF = FAR // 2


def dot(left, right, contract):
    return lax.dot_general(
        left, right, ((contract[:1], contract[1:]), ((), ())), preferred_element_type=F32
    )


def nn(left, right):
    return dot(left, right, (1, 0))


def nt(left, right):
    return dot(left, right, (1, 1))


def tn(left, right):
    return dot(left, right, (0, 0))


def split_pair(cells):
    low = lax.broadcasted_iota(jnp.int32, cells.shape, 1) < HD
    zero = jnp.zeros_like(cells)
    return jnp.concatenate([jnp.where(low, cells, zero), jnp.where(low, zero, cells)], axis=0)


def lanes(pair):
    return slice(pair * 2 * HD, (pair + 1) * 2 * HD)


EDGE = REACH * BLK


def chunk(base, count, which):
    return pl.ds(base * 4 + which, count, stride=4)


def virtual_sums_kernel(
    k_ref, v_ref, vq_ref, vg_ref, out_ref, to_left_ref, to_right_ref, held, sem
):
    loads = [
        pltpu.make_async_copy(ref, held.at[which], sem.at[which])
        for which, ref in enumerate((k_ref, v_ref))
    ]
    for copy in loads:
        copy.start()
    copies = []
    for which in range(2):
        loads[which].wait()
        for start, ref in ((0, to_left_ref), (ROWS - EDGE, to_right_ref)):
            copies.append(
                pltpu.make_async_copy(
                    held.at[which, pl.ds(start, EDGE)], ref.at[which], sem.at[2 + len(copies)]
                )
            )
            copies[-1].start()
    for pair in range(PAIRS):
        sl = lanes(pair)
        keys, values = held[0, :, sl], held[1, :, sl]
        wq = split_pair(vq_ref[:, sl] * SCALE).astype(BF16)
        wg = split_pair(vg_ref[:, sl])
        scores = nt(keys, wq)
        top = jnp.max(scores, axis=0, keepdims=True)
        p = jnp.exp(scores - top)
        total = jnp.sum(p, axis=0, keepdims=True)
        gv = nt(values, wg)
        centre = jnp.sum(p * gv, axis=0, keepdims=True) / total
        rounded = p.astype(BF16)
        weighted = tn(rounded, values)
        first = tn((p * (gv - centre)).astype(BF16), keys)
        second = tn(rounded, keys)
        stats = jnp.concatenate(
            [top, total, centre, jnp.zeros((2 * VC - 3, 2 * VC), F32)], axis=0
        ).T
        for half in range(2):
            rows = slice(half * VC, (half + 1) * VC)
            part = slice(half * HD, (half + 1) * HD)
            at = (pair % 2) * 2 * VC + half * VC
            base = (pair // 2) * 2
            out_ref[chunk(at, VC, base), :] = jnp.concatenate(
                [weighted[rows, part], stats[rows, :HD]], axis=1
            )
            out_ref[chunk(at, VC, base + 1), :] = jnp.concatenate(
                [first[rows, part], second[rows, part]], axis=1
            )
    for copy in copies:
        copy.wait()


def wanted_row(requests, member):
    return pl.multiple_of((requests[member % OFFS][member] % NB) * BLK, BLK)


def pack_kernel(*refs):
    requests, owned, outs, sem = refs[:OFFS], refs[OFFS : OFFS + 2], refs[OFFS + 2 : -1], refs[-1]
    copies = []
    for member in range(FAR):
        for which, ref in enumerate(owned):
            copies.append(
                pltpu.make_async_copy(
                    ref.at[pl.ds(wanted_row(requests, member), BLK)],
                    outs[member].at[which],
                    sem.at[len(copies)],
                )
            )
            copies[-1].start()
    for copy in copies:
        copy.wait()


def virtual_merge_kernel(parts_ref, sums_a_ref, sums_b_ref, vg_ref, out_ref, results_ref):
    devices = parts_ref.shape[0] // 4
    me = lax.axis_index("nodes")
    lane = lax.broadcasted_iota(jnp.int32, (1, 128), 1)
    stats = jnp.zeros((1, 128), F32)
    results = []
    for n in range(2):
        at = pl.ds(n, devices, stride=2)
        out_ref[chunk(0, devices, 1 + n), :] = sums_a_ref[at, :] + sums_b_ref[at, :]
    query = lax.broadcasted_iota(jnp.int32, vg_ref.shape, 0)
    grads = jnp.sum(jnp.where(query == me % VC, vg_ref[...].astype(F32), 0.0), axis=0, keepdims=True)
    for c in range(2):
        grad_row = jnp.zeros((1, HD), F32)
        for head in range(HEADS // 2):
            at = (c * (HEADS // 2) + head) * HD
            grad_row = jnp.where(me // VC == head, grads[:, at : at + HD], grad_row)
        one = parts_ref[chunk(0, devices, 2 * c), :]
        two = parts_ref[chunk(0, devices, 2 * c + 1), :]
        top, total, centre = (one[:, HD + n : HD + n + 1] for n in range(3))
        highest = jnp.max(top, axis=0, keepdims=True)
        scale = jnp.exp(top - highest)
        all_total = jnp.sum(scale * total, axis=0, keepdims=True)
        output = jnp.sum(scale * one[:, :HD], axis=0, keepdims=True) / all_total
        output = output.astype(BF16).astype(F32)
        vdelta = jnp.sum(grad_row * output, axis=1, keepdims=True)
        grad = jnp.sum(
            scale * (two[:, :HD] + (centre - vdelta) * two[:, HD:]), axis=0, keepdims=True
        )
        grad = grad * (SCALE / all_total)
        for n, cell in enumerate((highest, all_total, vdelta)):
            stats = jnp.where(lane == c * HD + n, cell, stats)
        results.append(jnp.concatenate([output, grad], axis=1))
    out_ref[chunk(0, devices, 0), :] = jnp.broadcast_to(stats, (devices, 128))
    out_ref[chunk(0, devices, 3), :] = jnp.zeros((devices, 128), F32)
    results_ref[...] = jnp.concatenate([*results, jnp.zeros((6, 128), F32)], axis=0)


def block_place(cols_ref, b, e):
    return pl.multiple_of((cols_ref[b, e] - cols_ref[0, 0] + REACH) * BLK, BLK)


def edges_kernel(
    first_block,
    cols_ref,
    bits_ref,
    q_ref,
    g_ref,
    k_ref,
    v_ref,
    left_ref,
    right_ref,
    vk_ref,
    vv_ref,
    *rest,
):
    fars, rest = rest[:HALF], rest[-13 - HALF + 1 :]
    out_ref, ds_ref, p_ref, sums_ref = rest[:4]
    far_outs = rest[4 : 4 + HALF]
    band, far, far_grads, cat, bias, virt_acc, sem, out_sem = rest[4 + HALF :]
    step = pl.program_id(0)
    b = first_block + step

    @pl.when(step == 0)
    def start():
        arrivals = [
            pltpu.make_async_copy(fars[m], far.at[m], sem.at[m]) for m in range(HALF)
        ]
        for copy in arrivals:
            copy.start()
        for which, own in enumerate((k_ref, v_ref)):
            band[which, 0:EDGE] = left_ref[which]
            band[which, EDGE : EDGE + ROWS] = own[...]
            band[which, EDGE + ROWS : 2 * EDGE + ROWS] = right_ref[which]
        cat[0, COLS:ALL] = vk_ref[...]
        cat[1, COLS:ALL] = vv_ref[...]
        bias[COLS:ALL] = jnp.zeros((VC, 2 * BLK), F32)
        virt_acc[...] = jnp.zeros(virt_acc.shape, F32)
        for copy in arrivals:
            copy.wait()

    row_lane = lax.broadcasted_iota(jnp.int32, (1, 2 * BLK), 1) % BLK
    col_row = lax.broadcasted_iota(jnp.int32, (BLK, 2 * BLK), 0)

    def pick(words, index):
        word = index // 32
        chosen = jnp.where(
            word == 0, words[0], jnp.where(word == 1, words[1], jnp.where(word == 2, words[2], words[3]))
        )
        return (jnp.right_shift(chosen, index % 32) & 1) > 0

    for e in range(LOC + EXP):
        at = slice(e * BLK, (e + 1) * BLK)
        for which in range(2):
            if e < LOC:
                cat[which, at] = band[which, pl.ds(block_place(cols_ref, b, e), BLK)]
            else:
                cat[which, at] = far[step * EXP + (e - LOC), which]
        words = [bits_ref[b, e, w] for w in range(8)]
        linked = pick(words[:4], row_lane) & pick(words[4:], col_row)
        bias[at] = jnp.where(linked, 0.0, MASKED)
    for pair in range(PAIRS):
        sl = lanes(pair)
        grad = g_ref[:, sl]
        wq = split_pair(q_ref[:, sl] * SCALE).astype(BF16)
        wg = split_pair(grad)
        keys, values = cat[0, :, sl], cat[1, :, sl]
        scores = nt(keys, wq) + bias[...]
        top = jnp.max(scores, axis=0, keepdims=True)
        w = jnp.exp(scores - top)
        total = jnp.sum(w, axis=0, keepdims=True)
        p = w * (1.0 / total)
        rounded = p.astype(BF16)
        p_ref[0, pair] = rounded[: LOC * BLK]
        mixed = tn(values, rounded)
        output = jnp.concatenate([mixed[:HD, :BLK], mixed[HD:, BLK:]], axis=0)
        output = output.astype(BF16).astype(F32)
        out_ref[:, sl] = output.T.astype(BF16)
        product = output * grad.astype(F32).T
        delta = jnp.concatenate(
            [
                jnp.sum(product[:HD], axis=0, keepdims=True),
                jnp.sum(product[HD:], axis=0, keepdims=True),
            ],
            axis=1,
        )
        ds = (p * (nt(values, wg) - delta)).astype(BF16)
        ds_ref[0, pair] = ds
        for which, grads in enumerate((nn(ds[LOC * BLK :], wq), nn(rounded[LOC * BLK :], wg))):
            for e in range(EXP):
                far_grads[step * EXP + e, which, :, sl] = grads[e * BLK : (e + 1) * BLK].astype(BF16)
            virt_acc[which * PAIRS + pair] += grads[EXP * BLK :]

    leaving = [
        pltpu.make_async_copy(far_grads.at[m], far_outs[m], out_sem.at[m]) for m in range(HALF)
    ]
    for row in range(HALF // EXP):

        @pl.when(step == row)
        def send():
            for e in range(EXP):
                leaving[row * EXP + e].start()

    @pl.when(step == HALF // EXP - 1)
    def finish():
        for part in range(2 * PAIRS):
            sums_ref[part * VC : (part + 1) * VC] = virt_acc[part]
        for copy in leaving:
            copy.wait()


def gradients_kernel(
    cols_ref,
    q_ref,
    g_ref,
    ds_ref,
    p_ref,
    k_ref,
    left_ref,
    right_ref,
    vk_ref,
    *rest,
):
    fars = rest[:FAR]
    gq_ref, own_ref, to_left_ref, to_right_ref, band, far, cat, acc, sem = rest[FAR:]
    b = pl.program_id(0)

    @pl.when(b == 0)
    def start():
        arrivals = [
            pltpu.make_async_copy(fars[m].at[0], far.at[m], sem.at[m])
            for m in range(FAR)
        ]
        for copy in arrivals:
            copy.start()
        band[0:EDGE] = left_ref[0]
        band[EDGE : EDGE + ROWS] = k_ref[...]
        band[EDGE + ROWS : 2 * EDGE + ROWS] = right_ref[0]
        acc[...] = jnp.zeros(acc.shape, F32)
        cat[COLS:ALL] = vk_ref[...]
        for copy in arrivals:
            copy.wait()

    places = [block_place(cols_ref, b, e) for e in range(LOC)]
    for e in range(LOC + EXP):
        at = slice(e * BLK, (e + 1) * BLK)
        if e < LOC:
            cat[at] = band[pl.ds(places[e], BLK)]
        else:
            cat[at] = far[b * EXP + (e - LOC)]
    for pair in range(PAIRS):
        sl = lanes(pair)
        wq = split_pair(q_ref[:, sl] * SCALE).astype(BF16)
        wg = split_pair(g_ref[:, sl])
        ds = ds_ref[0, pair]
        mixed = tn(cat[:, sl], ds)
        grad_q = jnp.concatenate([mixed[:HD, :BLK], mixed[HD:, BLK:]], axis=0)
        gq_ref[:, sl] = (grad_q * SCALE).T.astype(BF16)
        for which, grads in enumerate((nn(ds[: LOC * BLK], wq), nn(p_ref[0, pair], wg))):
            for e in range(LOC):
                acc[which, pl.ds(places[e], BLK), sl] += grads[e * BLK : (e + 1) * BLK]

    @pl.when(b == NB - 1)
    def finish():
        for which in range(2):
            to_left_ref[which] = acc[which, 0:EDGE].astype(BF16)
            own_ref[which] = acc[which, EDGE : EDGE + ROWS]
            to_right_ref[which] = acc[which, EDGE + ROWS : 2 * EDGE + ROWS].astype(BF16)


def share_sum_kernel(parts_ref, results_ref, out_ref):
    devices = parts_ref.shape[0] // 4
    rows = [results_ref[0:2]]
    for n in range(2):
        rows.append(jnp.sum(parts_ref[chunk(0, devices, 1 + n), :], axis=0, keepdims=True))
    cells = jnp.concatenate(rows * 4, axis=0).astype(BF16)
    for at in range(0, out_ref.shape[0], 16):
        out_ref[at : at + 16] = cells


def share_place_kernel(shares_ref, vout_ref, gvq_ref, gvk_ref, gvv_ref, held, placed):
    held[...] = shares_ref[...].astype(F32)
    devices = shares_ref.shape[0] // 4
    for head in range(HEADS):
        cells = held[chunk((head % 4) * VC, VC, head // 4), :].astype(BF16)
        vout_ref[:, head * HD : (head + 1) * HD] = cells[:, :HD]
        gvq_ref[:, head * HD : (head + 1) * HD] = cells[:, HD:]
    for n in range(2):
        placed[pl.ds(n, devices, stride=2), :] = held[chunk(0, devices, 2 + n), :]
    for which, out in enumerate((gvk_ref, gvv_ref)):
        for pair in range(PAIRS):
            at = (which * PAIRS + pair) * VC
            out[:, lanes(pair)] = placed[at : at + VC, :].astype(BF16)


def collect_kernel(
    want0,
    want1,
    want2,
    want3,
    want4,
    k_ref,
    v_ref,
    vq_ref,
    vg_ref,
    all_ref,
    own_ref,
    from_left_ref,
    from_right_ref,
    *rest,
):
    fars = rest[:FAR]
    gk_ref, gv_ref, acc = rest[FAR:]
    for pair in range(PAIRS):
        sl = lanes(pair)
        stats = all_ref[chunk((pair % 2) * 2 * VC, 2 * VC, 0), :].T
        base = (pair // 2) * HD
        top, total, vdelta = (stats[base + n : base + n + 1] for n in range(3))
        wq = split_pair(vq_ref[:, sl] * SCALE).astype(BF16)
        wg = split_pair(vg_ref[:, sl])
        p = jnp.exp(nt(k_ref[:, sl], wq) - top) * (1.0 / total)
        da = p * (nt(v_ref[:, sl], wg) - vdelta)
        for which, grads in enumerate((nn(da.astype(BF16), wq), nn(p.astype(BF16), wg))):
            acc[which, 0:EDGE, sl] = (
                grads[0:EDGE] + own_ref[which, 0:EDGE, sl] + from_left_ref[which, :, sl].astype(F32)
            )
            acc[which, EDGE:ROWS, sl] = (
                grads[EDGE:] + own_ref[which, EDGE:ROWS, sl] + from_right_ref[which, :, sl].astype(F32)
            )
    for member in range(FAR):
        start = wanted_row((want0, want1, want2, want3, want4), member)
        for which in range(2):
            acc[which, pl.ds(start, BLK)] += fars[member][which].astype(F32)
    gk_ref[...] = acc[0].astype(BF16)
    gv_ref[...] = acc[1].astype(BF16)


def vmem(count):
    return [pl.BlockSpec(memory_space=pltpu.VMEM)] * count


def smem(count):
    return [pl.BlockSpec(memory_space=pltpu.SMEM)] * count


def anywhere(count):
    return [pl.BlockSpec(memory_space=pl.ANY)] * count


def by_block(*dims, first=0):
    return pl.BlockSpec(dims, lambda b: (b + first,) + (0,) * (len(dims) - 1))


def shape(dims, dtype):
    return jax.ShapeDtypeStruct(dims, dtype)


def call(kernel, name, ins, outs, out_specs, scratch=(), grid=(), flops=0, moved=0, limit=58, aliases=()):
    return pl.pallas_call(
        kernel,
        out_shape=outs,
        grid=grid,
        in_specs=ins,
        out_specs=out_specs,
        scratch_shapes=list(scratch),
        name=name,
        input_output_aliases=dict(aliases),
        cost_estimate=pl.CostEstimate(flops=flops, bytes_accessed=moved, transcendentals=0),
        compiler_params=pltpu.CompilerParams(vmem_limit_bytes=limit * 2**20),
    )


def shift(cells, distance):
    count = lax.axis_size("nodes")
    return lax.ppermute(cells, "nodes", [(i, (i + distance) % count) for i in range(count)])


def exchange(cells):
    return lax.all_to_all(cells, "nodes", 0, 0, tiled=True)


def on_device(
    node_q,
    node_k,
    node_v,
    node_grad,
    local_cols,
    expander_cols,
    edge_bits,
    virt_q,
    virt_k,
    virt_v,
    virt_grad,
):
    devices = lax.axis_size("nodes")
    distances = [devices >> (turn + 1) for turn in range(OFFS)]
    steps = [distances[member % OFFS] for member in range(FAR)]

    flat = expander_cols.reshape(FAR)
    requests = [shift(flat, distance) for distance in distances]
    parts, to_left, to_right = call(
        virtual_sums_kernel,
        "virtual_sums",
        anywhere(2) + vmem(2),
        [shape((devices * 4, 128), F32)] + [shape((2, EDGE, D), BF16)] * 2,
        vmem(1) + anywhere(2),
        [pltpu.VMEM((2, ROWS, D), BF16), pltpu.SemaphoreType.DMA((6,))],
        flops=1,
        moved=1,
    )(node_k, node_v, virt_q, virt_grad)
    from_left = shift(to_right, 1)
    from_right = shift(to_left, -1)
    requests[0], from_left, from_right = lax.optimization_barrier(
        (requests[0], from_left, from_right)
    )
    parts, requests = lax.optimization_barrier((parts, requests))
    parts = exchange(parts)
    one_block = shape((2, BLK, D), BF16)
    packed = call(
        pack_kernel,
        "pack_wanted",
        smem(OFFS) + vmem(2),
        [one_block] * FAR,
        anywhere(FAR),
        [pltpu.SemaphoreType.DMA((2 * FAR,))],
        flops=1,
        moved=1,
    )(*requests, node_k, node_v)
    far = [shift(cells, -step) for cells, step in zip(packed, steps)]

    edge_shapes = [
        shape((ROWS, D), BF16),
        shape((NB, PAIRS, ALL, 2 * BLK), BF16),
        shape((NB, PAIRS, LOC * BLK, 2 * BLK), BF16),
    ]
    earlier, sums, far_grads = [], [], []
    for half in range(2):
        first = half * (NB // 2)
        blocks = [
            by_block(BLK, D, first=first),
            by_block(1, PAIRS, ALL, 2 * BLK, first=first),
            by_block(1, PAIRS, LOC * BLK, 2 * BLK, first=first),
        ]
        outs = call(
            functools.partial(edges_kernel, first),
            "edges_first" if half == 0 else "edges_second",
            smem(2) + [blocks[0]] * 2 + vmem(6) + anywhere(HALF + len(earlier)),
            edge_shapes + [shape((devices * 2, 2 * HD), F32)] + [one_block] * HALF,
            blocks + vmem(1) + anywhere(HALF),
            [
                pltpu.VMEM((2, BAND * BLK, D), BF16),
                pltpu.VMEM((HALF, 2, BLK, D), BF16),
                pltpu.VMEM((HALF, 2, BLK, D), BF16),
                pltpu.VMEM((2, ALL, D), BF16),
                pltpu.VMEM((ALL, 2 * BLK), F32),
                pltpu.VMEM((2 * PAIRS, VC, 2 * HD), F32),
                pltpu.SemaphoreType.DMA((HALF,)),
                pltpu.SemaphoreType.DMA((HALF,)),
            ],
            grid=(NB // 2,),
            flops=1,
            moved=1,
            aliases=[(10 + HALF + n, n) for n in range(len(earlier))],
        )(
            local_cols,
            edge_bits,
            node_q,
            node_grad,
            node_k,
            node_v,
            from_left,
            from_right,
            virt_k,
            virt_v,
            *far[half * HALF : (half + 1) * HALF],
            *earlier,
        )
        earlier = outs[:3]
        sums.append(outs[3])
        far_grads.append(outs[4:])
    node_output, ds, p = earlier
    returned = [shift(cells, step) for cells, step in zip(far_grads[0], steps)]
    returned += [shift(cells, step) for cells, step in zip(far_grads[1], steps[HALF:])]

    grad_q, own, to_left, to_right = call(
        gradients_kernel,
        "gradients",
        smem(1)
        + [by_block(BLK, D)] * 2
        + [by_block(1, PAIRS, ALL, 2 * BLK), by_block(1, PAIRS, LOC * BLK, 2 * BLK)]
        + vmem(4)
        + anywhere(FAR),
        [
            shape((ROWS, D), BF16),
            shape((2, ROWS, D), F32),
            shape((2, EDGE, D), BF16),
            shape((2, EDGE, D), BF16),
        ],
        [by_block(BLK, D)] + vmem(3),
        [
            pltpu.VMEM((BAND * BLK, D), BF16),
            pltpu.VMEM((FAR, BLK, D), BF16),
            pltpu.VMEM((ALL, D), BF16),
            pltpu.VMEM((2, BAND * BLK, D), F32),
            pltpu.SemaphoreType.DMA((FAR,)),
        ],
        grid=(NB,),
        flops=1,
        moved=1,
    )(
        local_cols,
        node_q,
        node_grad,
        ds,
        p,
        node_k,
        from_left,
        from_right,
        virt_k,
        *far,
    )
    to_left, to_right, returned[HALF:] = lax.optimization_barrier(
        (to_left, to_right, returned[HALF:])
    )
    from_right_grads = shift(to_left, -1)
    from_left_grads = shift(to_right, 1)

    sums[1], returned[:HALF] = lax.optimization_barrier((sums[1], returned[:HALF]))
    merged, results = call(
        virtual_merge_kernel,
        "virtual_merge",
        vmem(4),
        [shape((devices * 4, 128), F32), shape((8, 128), F32)],
        vmem(2),
        flops=1,
        moved=1,
    )(parts, *sums, virt_grad)
    merged = exchange(merged)
    shares = call(
        share_sum_kernel,
        "share_sum",
        vmem(2),
        shape((devices * 4, 128), BF16),
        pl.BlockSpec(memory_space=pltpu.VMEM),
        flops=1,
        moved=1,
    )(merged, results)
    virtual_output, grad_vq, grad_vk, grad_vv = call(
        share_place_kernel,
        "share_place",
        vmem(1),
        [shape((VC, D), BF16)] * 4,
        vmem(4),
        [pltpu.VMEM((devices * 4, 128), F32), pltpu.VMEM((devices * 2, 128), F32)],
        flops=1,
        moved=1,
    )(exchange(shares))

    grad_k, grad_v = call(
        collect_kernel,
        "collect",
        smem(OFFS) + vmem(8 + FAR),
        [shape((ROWS, D), BF16)] * 2,
        vmem(2),
        [pltpu.VMEM((2, ROWS, D), F32)],
        flops=2 * ROWS * VC * D * 4,
        moved=7 * 2**20,
    )(
        *requests,
        node_k,
        node_v,
        virt_q,
        virt_grad,
        merged,
        own,
        from_left_grads,
        from_right_grads,
        *returned,
    )
    return node_output, virtual_output, grad_q, grad_k, grad_v, grad_vq, grad_vk, grad_vv


def solution(mesh):
    rows = P("nodes", None)
    return jax.shard_map(
        on_device,
        mesh=mesh,
        in_specs=(rows,) * 6 + (P("nodes", None, None),) + (P(),) * 4,
        out_specs=(rows, P(), rows, rows, rows, P(), P(), P()),
        check_vma=False,
    )
```
